32 devices in a mesh: rep: 2 (over x), fsdp: 4 (over y, core), tp: 4 (over z).
Axes of the slice: x: 2, y: 2, z: 4, core: 2. Of those that a mesh axis runs over, the one named last changes fastest.
Arguments:
- gate_up_master: float32 [2, 4096, 14336], P(None, 'fsdp', ('rep', 'tp')), may hold values from -0.09375 to 0.09375
- gate_up_moment: float32 [2, 4096, 14336], P(None, 'fsdp', ('rep', 'tp')), may hold values from -0.00018310547 to 0.00018310547
- gate_up_second: float32 [2, 4096, 14336], P(None, 'fsdp', ('rep', 'tp')), may hold values from 8.5149493e-10 to 8.51495e-09
- gate_up_grad: bfloat16 [2, 4096, 14336], P(None, 'fsdp', ('rep', 'tp')), may hold values from -8 to 8
- down_master: float32 [4096, 14336], P('fsdp', ('rep', 'tp')), may hold values from -0.046875 to 0.046875
- down_moment: float32 [4096, 14336], P('fsdp', ('rep', 'tp')), may hold values from -0.00018310547 to 0.00018310547
- down_second: float32 [4096, 14336], P('fsdp', ('rep', 'tp')), may hold values from 8.5149493e-10 to 8.51495e-09
- down_grad: bfloat16 [4096, 14336], P('fsdp', ('rep', 'tp')), may hold values from -8 to 8
- norm_gain: float32 [4096], replicated, may hold values from 0.1 to 1.9
- start_rows: bfloat16 [256, 4096], P(('rep', 'fsdp', 'tp')), may hold values from -6 to 6
- queries: bfloat16 [2, 256, 4096], P(None, ('rep', 'fsdp', 'tp')), may hold values from -6 to 6
- new_kv: bfloat16 [2, 256, 2, 1024], P(None, ('rep', 'fsdp', 'tp')), may hold values from -6 to 6
- kv_pool: bfloat16 [2048, 16, 2, 1024], P(('rep', 'fsdp', 'tp')), may hold values from -6 to 6
- page_table: int32 [256, 8], P(('rep', 'fsdp', 'tp')), may hold values from 0 to 63, as said below
- cache_len: int32 [256], P(('rep', 'fsdp', 'tp')), may hold values from 1 to 128, as said below
Outputs:
- final_rows: bfloat16 [256, 4096], P(('rep', 'fsdp', 'tp'))
The draws below stay inside these ranges and needn't reach their ends.
Inputs may be any that keep to these rules, and one draw needn't show every extreme that they name: `page_table`: within each aligned block of 8 rows, the entries name each of the 64 pages of that block exactly once. `cache_len`: some row has exactly 128 cached positions.
All inputs are finite; a program needn't handle non-finite values.
Results may differ from the reference program's by a relative error of at most 0.019.
Values may be sent and summed in bfloat16 or wider, within the bound.
A program may use at most 192 MiB of HBM per device.

```python
import math
import jax
import jax.numpy as jnp
from jax import lax

D = 4096
FF = 14336
HD = 128
KVH = 8
GROUP = 4
QH = 32
KVD = 1024
RD = 8
PAGE = 16
PPR = 8
CTX = 128
STEPS = 2
ROWS = 256
POOL_PAGES = 2048


def make_grad(key, stack):
    k_row, k_col, k_base = jax.random.split(key, 3)
    position = jnp.arange(D, dtype=jnp.float32) / (D - 1)
    col_position = jnp.arange(FF, dtype=jnp.float32) / (FF - 1)
    row_scale = (1.0 + 2.0 * position).reshape(1, D, 1) * jnp.exp(jnp.log(10.0) * jax.random.uniform(k_row, (stack, D, 1)))
    col_scale = (1.0 + 2.0 * col_position).reshape(1, 1, FF) * jnp.exp(jnp.log(10.0) * jax.random.uniform(k_col, (stack, 1, FF)))
    base = jax.random.normal(k_base, (stack, D, FF))
    size = 0.0002
    values = jnp.clip(size * row_scale * col_scale * base, -8.0, 8.0)
    return values.astype(jnp.bfloat16)


def draw_gate_up_grad(key, part):
    return make_grad(jax.random.fold_in(key, 11), 2)


def draw_down_grad(key, part):
    return make_grad(jax.random.fold_in(key, 12), 1)[0]


def draw_kv_pool(key, part):
    k_base = jax.random.fold_in(jax.random.fold_in(key, 21), 0)
    shape = (POOL_PAGES, PAGE, 2, KVD)
    base = jax.random.normal(k_base, shape)
    return jnp.clip(base, -6.0, 6.0).astype(jnp.bfloat16)


def draw_queries(key, part):
    k_base = jax.random.fold_in(jax.random.fold_in(key, 22), 0)
    shape = (STEPS, ROWS, QH, HD)
    base = jax.random.normal(k_base, shape)
    return jnp.clip(base, -6.0, 6.0).reshape(STEPS, ROWS, QH * HD).astype(jnp.bfloat16)


def draw_page_table(key, part):
    blocks = ROWS // RD
    keys = jax.random.split(jax.random.fold_in(key, 31), blocks)
    orders = jax.vmap(lambda k: jax.random.permutation(k, RD * PPR))(keys)
    return orders.reshape(ROWS, PPR).astype(jnp.int32)


def draw_cache_len(key, part):
    k_len, k_pick = jax.random.split(jax.random.fold_in(key, 41), 2)
    lengths = jax.random.randint(k_len, (ROWS,), 1, CTX + 1)
    chosen = jax.random.randint(k_pick, (), 0, ROWS)
    return jnp.where(jnp.arange(ROWS) == chosen, CTX, lengths).astype(jnp.int32)


def block_scale(stream_key, shape, cuts, smallest, top_value):
    factor_of, own = 1.0, jax.random.fold_in(stream_key, 6)
    for dim, parts in cuts:
        heights = jnp.exp(jax.random.uniform(jax.random.fold_in(own, dim), (parts,), jnp.float32, smallest / len(cuts), top_value / len(cuts)))
        factor_of = factor_of * jnp.repeat(heights, shape[dim] // parts).reshape([-1 if axis == dim else 1 for axis in range(len(shape))])
    return factor_of


def normal_values(stream_key, dims, scale, most, shards=(), kind=jnp.bfloat16):
    values = scale * jax.random.normal(stream_key, dims, jnp.float32)
    if shards:
        values = values * block_scale(stream_key, dims, shards, -0.22, 0.18)
    return jnp.clip(values, -most, most).astype(kind)


def setup_inputs(seed: int = 0) -> dict:
    key_list = jax.random.split(jax.random.key(seed), 16)
    gate_up_master = normal_values(key_list[0], (2, D, FF), D ** -0.5, 0.09375, ((1, 4), (2, 8)), jnp.float32)
    gate_up_moment = normal_values(key_list[1], (2, D, FF), (0.1 * (D * FF) ** -0.5), 0.00018310547, ((1, 4), (2, 8)), jnp.float32)
    gate_up_second = jnp.clip(jnp.exp(math.log(8.514949634275126e-09) - 2.3025851 * jax.random.uniform(key_list[2], (2, D, FF), jnp.float32) ** block_scale(key_list[2], (2, D, FF), ((1, 4), (2, 8)), -0.2, 0.2)), 8.514949301208219e-10, 8.514949634275126e-09)
    gate_up_grad = draw_gate_up_grad(jax.random.fold_in(key_list[15], 71), 0)
    down_master = normal_values(key_list[4], (D, FF), FF ** -0.5, 0.046875, ((0, 4), (1, 8)), jnp.float32)
    down_moment = normal_values(key_list[5], (D, FF), (0.1 * (D * FF) ** -0.5), 0.00018310547, ((0, 4), (1, 8)), jnp.float32)
    down_second = jnp.clip(jnp.exp(math.log(8.514949634275126e-09) - 2.3025851 * jax.random.uniform(key_list[6], (D, FF), jnp.float32) ** block_scale(key_list[6], (D, FF), ((0, 4), (1, 8)), -0.2, 0.2)), 8.514949301208219e-10, 8.514949634275126e-09)
    down_grad = draw_down_grad(jax.random.fold_in(key_list[15], 71), 0)
    norm_gain = jnp.clip(1.0 + 0.18 * jax.random.normal(key_list[8], (D,), jnp.float32), 0.1, 1.9)
    start_rows = normal_values(key_list[9], (ROWS, D), 1.0, 6.0, ((0, 32),))
    queries = draw_queries(jax.random.fold_in(key_list[15], 71), 0)
    new_kv = normal_values(key_list[11], (STEPS, ROWS, 2, KVD), 1.0, 6.0, ((1, 32),))
    kv_pool = draw_kv_pool(jax.random.fold_in(key_list[15], 71), 0)
    page_table = draw_page_table(jax.random.fold_in(key_list[15], 71), 0)
    cache_len = draw_cache_len(jax.random.fold_in(key_list[15], 71), 0)
    return {"gate_up_master": gate_up_master, "gate_up_moment": gate_up_moment, "gate_up_second": gate_up_second, "gate_up_grad": gate_up_grad, "down_master": down_master, "down_moment": down_moment, "down_second": down_second, "down_grad": down_grad, "norm_gain": norm_gain, "start_rows": start_rows, "queries": queries, "new_kv": new_kv, "kv_pool": kv_pool, "page_table": page_table, "cache_len": cache_len}


beta_one = 0.9
beta_two = 0.95
adam_eps = 1e-08
adam_time = 100.0
norm_eps = 1e-05

def adam_new(master, moment, second, grad, clip):
    learn_rate = 2.0 / D ** 0.5
    g = grad.astype(jnp.float32) * clip
    m = beta_one * moment + (1.0 - beta_one) * g
    v = beta_two * second + (1.0 - beta_two) * g * g
    first_fix = 1.0 - beta_one ** adam_time
    second_fix = 1.0 - beta_two ** adam_time
    return (master - learn_rate * (m / first_fix) / (jnp.sqrt(v / second_fix) + adam_eps)).astype(jnp.bfloat16)

def attend(query, keys, values, valid, fresh_k, fresh_v, step):
    scale = query.shape[-1] ** (-0.5)
    old = jnp.einsum('rjgh,rcjh->rjgc', query.astype(jnp.float32), keys.astype(jnp.float32)) * scale
    old = jnp.where(valid[:, None, None, :], old, -1e+30)
    new = jnp.einsum('rjgh,srjh->rjgs', query.astype(jnp.float32), fresh_k.astype(jnp.float32)) * scale
    allowed = jnp.arange(fresh_k.shape[0]) <= step
    new = jnp.where(allowed[None, None, None, :], new, -1e+30)
    top = jnp.maximum(lax.optimization_barrier(jnp.max(old, axis=-1, keepdims=True)), lax.optimization_barrier(jnp.max(new, axis=-1, keepdims=True)))
    exp_old = jnp.exp(old - top)
    exp_new = jnp.exp(new - top)
    total = lax.optimization_barrier(jnp.sum(exp_old, axis=-1, keepdims=True)) + lax.optimization_barrier(jnp.sum(exp_new, axis=-1, keepdims=True))
    prob_old = (exp_old / total).astype(jnp.bfloat16)
    prob_new = (exp_new / total).astype(jnp.bfloat16)
    out = jnp.einsum('rjgc,rcjh->rjgh', prob_old.astype(jnp.float32), values.astype(jnp.float32))
    out = out + jnp.einsum('rjgs,srjh->rjgh', prob_new.astype(jnp.float32), fresh_v.astype(jnp.float32))
    return out.reshape(out.shape[0], -1)

def reference(gate_up_master, gate_up_moment, gate_up_second, gate_up_grad, down_master, down_moment, down_second, down_grad, norm_gain, start_rows, queries, new_kv, kv_pool, page_table, cache_len):
    total = jnp.sum(jnp.square(gate_up_grad.astype(jnp.float32))) + jnp.sum(jnp.square(down_grad.astype(jnp.float32)))
    clip = jnp.minimum(1.0, 1.0 / jnp.sqrt(total))
    gate_up = adam_new(gate_up_master, gate_up_moment, gate_up_second, gate_up_grad, clip)
    down_t = adam_new(down_master, down_moment, down_second, down_grad, clip)
    owner = (jnp.arange(ROWS, dtype=jnp.int32) // RD).astype(jnp.int32)
    global_page = (owner[:, None] * (RD * PPR) + page_table).astype(jnp.int32)
    cache = kv_pool[global_page].reshape(ROWS, CTX, 2, KVH, HD)
    keys = cache[:, :, 0]
    values = cache[:, :, 1]
    valid = jnp.arange(CTX, dtype=jnp.int32)[None, :] < cache_len[:, None]
    fresh = new_kv.reshape(STEPS, ROWS, 2, KVH, HD)
    fresh_k = fresh[:, :, 0]
    fresh_v = fresh[:, :, 1]
    rows = start_rows
    for step in range(STEPS):
        query = queries[step].reshape(ROWS, KVH, GROUP, HD)
        attended = attend(query, keys, values, valid, fresh_k, fresh_v, step)
        mixed = (rows.astype(jnp.float32) + attended).astype(jnp.bfloat16)
        mixed_f = mixed.astype(jnp.float32)
        normed = (mixed_f * lax.rsqrt(lax.optimization_barrier(jnp.mean(mixed_f * mixed_f, axis=-1, keepdims=True)) + norm_eps) * norm_gain).astype(jnp.bfloat16)
        gate = jnp.dot(normed, gate_up[0], preferred_element_type=jnp.float32)
        upper = jnp.dot(normed, gate_up[1], preferred_element_type=jnp.float32)
        hidden = (jax.nn.silu(gate) * upper).astype(jnp.bfloat16)
        summed = jnp.dot(hidden, down_t.T, preferred_element_type=jnp.float32)
        rows = (mixed_f + summed).astype(jnp.bfloat16)
    return rows
```

```python
import functools

import jax
import jax.numpy as jnp
from jax import lax
from jax.experimental import pallas as pl
from jax.experimental.pallas import tpu as pltpu
from jax.sharding import PartitionSpec as P

HD = 128
FULL_WIDTH = 4096
MESH = pl.DeviceIdType.MESH

beta_one = 0.9
beta_two = 0.95
adam_eps = 1e-08
adam_time = 100.0
norm_eps = 1e-05

TILE = 256
CHUNK = 128
SUB = 16
SLOTS = 4


def attend_all(queries, kv_pool, page_table, cache_len, new_kv):
    steps, rows, _ = queries.shape
    pages, page, _, kv_width = kv_pool.shape
    heads = kv_width // HD
    scale = HD**-0.5
    pool = kv_pool.reshape(pages * page, 2, heads, HD)
    keys, values = pool[:, 0], pool[:, 1]
    slot = jnp.arange(page_table.shape[1], dtype=jnp.int32) * page
    place = slot[None, :, None, None] + jnp.arange(page, dtype=jnp.int32)
    named = page_table[:, :, None] == jnp.arange(pages, dtype=jnp.int32)
    valid = named[..., None] & (place < cache_len[:, None, None, None])
    valid = jnp.any(valid, axis=1).reshape(rows, pages * page)
    fresh = new_kv.reshape(steps, rows, 2, heads, HD)
    fresh_k, fresh_v = fresh[:, :, 0], fresh[:, :, 1]
    query = queries.reshape(steps, rows, heads, -1, HD)
    old = jnp.einsum("srjgh,cjh->jsrgc", query, keys, preferred_element_type=jnp.float32) * scale
    old = jnp.where(valid[None, None, :, None, :], old, -1e30)
    new = jnp.einsum("srjgh,trjh->jsrgt", query, fresh_k, preferred_element_type=jnp.float32) * scale
    allowed = jnp.arange(steps)[None, :] <= jnp.arange(steps)[:, None]
    new = jnp.where(allowed[None, :, None, None, :], new, -1e30)
    top = jnp.maximum(jnp.max(old, axis=-1, keepdims=True), jnp.max(new, axis=-1, keepdims=True))
    exp_old = jnp.exp(old - top)
    exp_new = jnp.exp(new - top)
    total = jnp.sum(exp_old, axis=-1, keepdims=True) + jnp.sum(exp_new, axis=-1, keepdims=True)
    prob_old = (exp_old / total).astype(jnp.bfloat16)
    prob_new = (exp_new / total).astype(jnp.bfloat16)
    out = jnp.einsum("jsrgc,cjh->srjgh", prob_old, values, preferred_element_type=jnp.float32)
    out = out + jnp.einsum("jsrgt,trjh->srjgh", prob_new, fresh_v, preferred_element_type=jnp.float32)
    return out.reshape(steps, rows, -1)


def block_kernel(
    n_rep,
    n_fsdp,
    n_tp,
    gu_master,
    gu_moment,
    gu_second,
    gu_grad,
    d_master,
    d_moment,
    d_second,
    d_grad,
    pieces,
    gain,
    out,
    weights,
    slots,
    got_pieces,
    sums,
    x,
    own,
    core_out,
    core_in,
    y_out,
    y_in,
    hid,
    acc,
    down_out,
    down_in,
    squares,
    mixed,
    fin_out,
    fin_in,
    grad_sem,
    slot_sem,
    f_send,
    f_recv,
    s_send,
    s_recv,
    x_send,
    x_recv,
    core_send,
    core_recv,
    y_send,
    y_recv,
    h_send,
    h_recv,
    hc_send,
    hc_recv,
    d_send,
    d_recv,
):
    n_group = n_rep * n_tp
    members = n_fsdp // 2
    depth, cols = d_grad.shape
    tiles = cols // TILE
    steps = pieces.shape[1] // 8 - 1
    half = x.shape[1] * x.shape[2]
    part = half // members

    r = lax.axis_index("rep")
    f = lax.axis_index("fsdp")
    t = lax.axis_index("tp")
    g = r * n_tp + t
    c = lax.rem(f, 2)
    m = f // 2

    def f_dev(k):
        return (r, lax.rem(f + k, n_fsdp), t)

    def g_dev(k):
        there = lax.rem(g + k, n_group)
        return (there // n_tp, f, lax.rem(there, n_tp))

    def m_dev(k):
        return (r, lax.rem(m + k, members) * 2 + c, t)

    sibling = (r, m * 2 + 1 - c, t)

    barrier = pltpu.get_barrier_semaphore()
    for k in range(1, n_fsdp):
        pl.semaphore_signal(barrier, inc=1, device_id=f_dev(k), device_id_type=MESH)
    for k in range(1, n_group):
        pl.semaphore_signal(barrier, inc=1, device_id=g_dev(k), device_id_type=MESH)

    stacks = (
        (gu_master.at[0], gu_moment.at[0], gu_second.at[0], gu_grad.at[0]),
        (gu_master.at[1], gu_moment.at[1], gu_second.at[1], gu_grad.at[1]),
        (d_master, d_moment, d_second, d_grad),
    )
    per = depth // CHUNK
    chunks = [(s, i) for s in range(3) for i in range(per)]

    def grad_copy(n):
        s, i = chunks[n]
        rows = pl.ds(i * CHUNK, CHUNK)
        return pltpu.make_async_copy(stacks[s][3].at[rows], weights.at[s, rows], grad_sem.at[n])

    def state_copies(n):
        s, i = chunks[n]
        rows = pl.ds(i * CHUNK, CHUNK)
        slot = n % SLOTS
        return [
            pltpu.make_async_copy(stacks[s][a].at[rows], slots.at[slot, a], slot_sem.at[slot, a])
            for a in range(3)
        ]

    for n in range(len(chunks)):
        grad_copy(n).start()
    for n in range(min(SLOTS, len(chunks))):
        for copy in state_copies(n):
            copy.start()

    pl.semaphore_wait(barrier, n_fsdp + n_group - 2)

    def remote(src, dst, send, recv, dev):
        return pltpu.make_async_remote_copy(
            src_ref=src, dst_ref=dst, send_sem=send, recv_sem=recv, device_id=dev, device_id_type=MESH
        )

    piece_copies = []
    for k in range(1, n_fsdp):
        there = lax.rem(f + k, n_fsdp)
        copy = remote(pieces.at[there], got_pieces.at[k], f_send.at[k], f_recv.at[k], f_dev(k))
        copy.start()
        piece_copies.append(copy)
    got_pieces[0] = pieces[f]

    total = jnp.zeros((8, cols), jnp.float32)
    for n in range(len(chunks)):
        grad_copy(n).wait()
        s, i = chunks[n]

        def square(b, run, s=s, i=i):
            rows = pl.ds(pl.multiple_of(i * CHUNK + b * SUB, SUB), SUB)
            v = weights[s, rows, :].astype(jnp.float32)
            v = v * v
            return run + (v[:8] + v[8:])

        total = lax.fori_loop(0, CHUNK // SUB, square, total)
    tile_sum = total[:, :128]
    for b in range(1, cols // 128):
        tile_sum = tile_sum + total[:, b * 128 : (b + 1) * 128]

    def sum_over(value, base, n, dev):
        sums[base] = value
        copies = []
        for k in range(1, n):
            copy = remote(sums.at[base], sums.at[base + k], s_send.at[base + k], s_recv.at[base + k], dev(k))
            copy.start()
            copies.append(copy)
        for copy in copies:
            copy.wait()
        for k in range(1, n):
            value = value + sums[base + k]
        return value

    tile_sum = sum_over(tile_sum, 0, n_fsdp, f_dev)

    for copy in piece_copies:
        copy.wait()

    def piece(a):
        blocks = [None] * n_fsdp
        at = pl.ds(a * 8, 8)
        for k in range(n_fsdp):
            blocks[k] = got_pieces[lax.rem(f - k + n_fsdp, n_fsdp), at, :]
        return jnp.concatenate(blocks, axis=0)

    x[0, 0] = piece(0).astype(jnp.bfloat16)
    mixed[...] = piece(1)

    def send_x():
        copies = []
        for k in range(1, n_group):
            at = x.at[k // x.shape[1], k % x.shape[1]]
            copy = remote(x.at[0, 0], at, x_send.at[k], x_recv.at[k], g_dev(k))
            copy.start()
            copies.append(copy)
        return copies

    tile_sum = sum_over(tile_sum, n_fsdp, n_group, g_dev)
    x_copies = send_x()
    clip = jnp.minimum(1.0, lax.rsqrt(jnp.sum(tile_sum, keepdims=True)))

    rate = 2.0 / FULL_WIDTH**0.5 / (1.0 - beta_one**adam_time)
    keep_m = rate * beta_one
    add_m = rate * (1.0 - beta_one)
    second_fix = 1.0 - beta_two**adam_time
    keep_v = beta_two / second_fix
    add_v = (1.0 - beta_two) / second_fix
    for n in range(len(chunks)):
        s, i = chunks[n]
        slot = n % SLOTS
        for copy in state_copies(n):
            copy.wait()

        def update(b, carry, s=s, i=i, slot=slot):
            at = pl.ds(pl.multiple_of(b * SUB, SUB), SUB)
            rows = pl.ds(pl.multiple_of(i * CHUNK + b * SUB, SUB), SUB)
            grad = weights[s, rows, :].astype(jnp.float32) * clip
            first = keep_m * slots[slot, 1, at, :] + add_m * grad
            second = keep_v * slots[slot, 2, at, :] + add_v * (grad * grad)
            new = slots[slot, 0, at, :] - first / (jnp.sqrt(second) + adam_eps)
            weights[s, rows, :] = new.astype(jnp.bfloat16)
            return carry

        lax.fori_loop(0, CHUNK // SUB, update, 0)
        if n + SLOTS < len(chunks):
            for copy in state_copies(n + SLOTS):
                copy.start()

    for copy in x_copies:
        copy.wait()

    for step in range(steps):

        def core_copy(j):
            return remote(core_out.at[j], core_in.at[j], core_send.at[j], core_recv.at[j], sibling)

        def y_copy(j, k):
            there = lax.rem(m + k, members)
            return remote(
                y_out.at[j, there], y_in.at[j, k - 1], y_send.at[j, k - 1], y_recv.at[j, k - 1], m_dev(k)
            )

        def h_copy(j, k):
            return remote(
                hid.at[j, c, m], hid.at[j, c, m], h_send.at[j, k - 1], h_recv.at[j, k - 1], m_dev(k)
            )

        def h_arrival(j, k):
            there = lax.rem(m - k + members, members)
            return remote(
                hid.at[j, c, m], hid.at[j, c, there], h_send.at[j, k - 1], h_recv.at[j, k - 1], m_dev(k)
            )

        def hc_copy(j):
            return remote(hid.at[j, c], hid.at[j, c], hc_send.at[j], hc_recv.at[j], sibling)

        def hc_arrival(j):
            return remote(hid.at[j, c], hid.at[j, 1 - c], hc_send.at[j], hc_recv.at[j], sibling)

        def multiply(j):
            at = pl.ds(pl.multiple_of(j * TILE, TILE), TILE)
            theirs = x[1 - c].reshape(half, depth)
            mine = x[c].reshape(half, depth)
            both = jnp.concatenate([theirs, mine], axis=0)
            for a in range(2):
                y = jnp.dot(both, weights[a, :, at], preferred_element_type=jnp.float32)
                core_out[j, :, a * TILE : (a + 1) * TILE] = y[:half].astype(jnp.bfloat16)
                own[j, :, a * TILE : (a + 1) * TILE] = y[half:]
            core_copy(j).start()

        def add_core(j):
            core_copy(j).wait()
            y = own[j] + core_in[j].astype(jnp.float32)
            own[j] = y
            y_out[j] = y.astype(jnp.bfloat16).reshape(members, part, 2 * TILE)
            for k in range(1, members):
                y_copy(j, k).start()

        def first_stage(j, carry):
            multiply(j)

            @pl.when(j > 0)
            def _():
                add_core(j - 1)

            return carry

        lax.fori_loop(0, tiles, first_stage, 0)
        add_core(tiles - 1)

        def second_stage(j, carry):
            y = own[j, pl.ds(pl.multiple_of(m * part, part), part), :]
            for k in range(1, members):
                y_copy(j, k).wait()
                y = y + y_in[j, k - 1].astype(jnp.float32)
            gate, upper = y[:, :TILE], y[:, TILE:]
            hid[j, c, m] = (gate * jax.nn.sigmoid(gate) * upper).astype(jnp.bfloat16)
            for k in range(1, members):
                h_copy(j, k).start()
            return carry

        lax.fori_loop(0, tiles, second_stage, 0)

        def third_stage(j, carry):
            for k in range(1, members):
                h_copy(j, k).wait_send()
                h_arrival(j, k).wait_recv()
            hc_copy(j).start()
            return carry

        lax.fori_loop(0, tiles, third_stage, 0)

        acc[...] = jnp.zeros_like(acc)

        def fourth_stage(j, carry):
            hc_copy(j).wait_send()
            hc_arrival(j).wait_recv()
            at = pl.ds(pl.multiple_of(j * TILE, TILE), TILE)
            acc[...] += lax.dot_general(
                hid[j].reshape(2 * half, TILE),
                weights[2, :, at],
                (((1,), (1,)), ((), ())),
                preferred_element_type=jnp.float32,
            )
            return carry

        lax.fori_loop(0, tiles, fourth_stage, 0)

        rows_of = acc.shape[0] // n_group
        copies = []
        for k in range(1, n_group):
            down_out[k] = acc[k * rows_of : (k + 1) * rows_of, :].astype(jnp.bfloat16)
            copy = remote(
                down_out.at[k], down_in.at[k], d_send.at[k], d_recv.at[k], g_dev(n_group - k)
            )
            copy.start()
            copies.append(copy)
        summed = acc[:rows_of, :]
        for k in range(1, n_group):
            copies[k - 1].wait()
            summed = summed + down_in[k].astype(jnp.float32)
        rows = (mixed[...] + summed).astype(jnp.bfloat16).astype(jnp.float32)

        if step < steps - 1:
            blend = (rows + piece(2 + step)).astype(jnp.bfloat16).astype(jnp.float32)
            mixed[...] = blend
            local = jnp.sum(blend * blend, axis=1, keepdims=True)
            squares[0] = jnp.broadcast_to(local, squares.shape[1:])
            copies = []
            for k in range(1, n_fsdp):
                copy = remote(squares.at[0], squares.at[k], f_send.at[k], f_recv.at[k], f_dev(k))
                copy.start()
                copies.append(copy)
            for copy in copies:
                copy.wait()
            whole = squares[0]
            for k in range(1, n_fsdp):
                whole = whole + squares[k]
            factor = lax.rsqrt(whole[:, :1] / (depth * n_fsdp) + norm_eps)
            x[0, 0] = (mixed[...] * factor * gain[...]).astype(jnp.bfloat16)
            for copy in send_x():
                copy.wait()
        else:
            for k in range(n_fsdp):
                fin_out[k] = rows[k * 8 : (k + 1) * 8, :]
            copies = []
            for k in range(1, n_fsdp):
                there = lax.rem(f + k, n_fsdp)
                copy = remote(fin_out.at[there], fin_in.at[k], f_send.at[k], f_recv.at[k], f_dev(k))
                copy.start()
                copies.append(copy)
            out[f] = fin_out[f]
            for k in range(1, n_fsdp):
                copies[k - 1].wait()
                out[lax.rem(f - k + n_fsdp, n_fsdp)] = fin_in[k]


def shards(
    gate_up_master,
    gate_up_moment,
    gate_up_second,
    gate_up_grad,
    down_master,
    down_moment,
    down_second,
    down_grad,
    norm_gain,
    start_rows,
    queries,
    new_kv,
    kv_pool,
    page_table,
    cache_len,
):
    n_rep, n_fsdp, n_tp = (lax.axis_size(a) for a in ("rep", "fsdp", "tp"))
    n_group = n_rep * n_tp
    depth, cols = down_grad.shape
    local_rows, width = start_rows.shape
    steps = queries.shape[0]
    tiles = cols // TILE
    members = n_fsdp // 2
    block = local_rows * n_fsdp
    all_rows = block * n_group
    half = all_rows // 2

    attended = attend_all(queries, kv_pool, page_table, cache_len, new_kv)
    mixed = (start_rows.astype(jnp.float32) + attended[0]).astype(jnp.bfloat16).astype(jnp.float32)
    normed = mixed * lax.rsqrt(jnp.mean(mixed * mixed, axis=-1, keepdims=True) + norm_eps) * norm_gain
    pieces = jnp.concatenate([normed[None], mixed[None], attended[1:]], axis=0)
    pieces = pieces.reshape(steps + 1, local_rows, n_fsdp, depth).transpose(2, 0, 1, 3)
    pieces = pieces.reshape(n_fsdp, (steps + 1) * local_rows, depth)
    gain = lax.dynamic_index_in_dim(norm_gain.reshape(n_fsdp, 1, depth), lax.axis_index("fsdp"), 0, False)

    n_chunks = 3 * (depth // CHUNK)
    bf16, f32 = jnp.bfloat16, jnp.float32
    dma = pltpu.SemaphoreType.DMA
    final = pl.pallas_call(
        functools.partial(block_kernel, n_rep, n_fsdp, n_tp),
        out_shape=jax.ShapeDtypeStruct((n_fsdp, local_rows, depth), f32),
        in_specs=[pl.BlockSpec(memory_space=pl.ANY)] * 8 + [pl.BlockSpec(memory_space=pltpu.VMEM)] * 2,
        out_specs=pl.BlockSpec(memory_space=pltpu.VMEM),
        scratch_shapes=[
            pltpu.VMEM((3, depth, cols), bf16),
            pltpu.VMEM((SLOTS, 3, CHUNK, cols), f32),
            pltpu.VMEM((n_fsdp, (steps + 1) * local_rows, depth), f32),
            pltpu.VMEM((n_fsdp + n_group, 8, 128), f32),
            pltpu.VMEM((2, n_group // 2, block, depth), bf16),
            pltpu.VMEM((tiles, half, 2 * TILE), f32),
            pltpu.VMEM((tiles, half, 2 * TILE), bf16),
            pltpu.VMEM((tiles, half, 2 * TILE), bf16),
            pltpu.VMEM((tiles, members, half // members, 2 * TILE), bf16),
            pltpu.VMEM((tiles, members - 1, half // members, 2 * TILE), bf16),
            pltpu.VMEM((tiles, 2, members, half // members, TILE), bf16),
            pltpu.VMEM((all_rows, depth), f32),
            pltpu.VMEM((n_group, block, depth), bf16),
            pltpu.VMEM((n_group, block, depth), bf16),
            pltpu.VMEM((n_fsdp, block, 128), f32),
            pltpu.VMEM((block, depth), f32),
            pltpu.VMEM((n_fsdp, local_rows, depth), f32),
            pltpu.VMEM((n_fsdp, local_rows, depth), f32),
            dma((n_chunks,)),
            dma((SLOTS, 3)),
            dma((n_fsdp,)),
            dma((n_fsdp,)),
            dma((n_fsdp + n_group,)),
            dma((n_fsdp + n_group,)),
            dma((n_group,)),
            dma((n_group,)),
            dma((tiles,)),
            dma((tiles,)),
            dma((tiles, members - 1)),
            dma((tiles, members - 1)),
            dma((tiles, members - 1)),
            dma((tiles, members - 1)),
            dma((tiles,)),
            dma((tiles,)),
            dma((n_group,)),
            dma((n_group,)),
        ],
        compiler_params=pltpu.CompilerParams(
            collective_id=0, has_side_effects=True, vmem_limit_bytes=60 * 2**20
        ),
        cost_estimate=pl.CostEstimate(
            flops=2 * steps * all_rows * 3 * depth * cols,
            bytes_accessed=3 * depth * cols * 14,
            transcendentals=3 * depth * cols,
        ),
        name="update_and_decode",
    )(
        gate_up_master,
        gate_up_moment,
        gate_up_second,
        gate_up_grad,
        down_master,
        down_moment,
        down_second,
        down_grad,
        pieces,
        gain,
    )
    return final.transpose(1, 0, 2).reshape(local_rows, width).astype(jnp.bfloat16)


def solution(mesh):
    in_specs = (
        P(None, "fsdp", ("rep", "tp")),
        P(None, "fsdp", ("rep", "tp")),
        P(None, "fsdp", ("rep", "tp")),
        P(None, "fsdp", ("rep", "tp")),
        P("fsdp", ("rep", "tp")),
        P("fsdp", ("rep", "tp")),
        P("fsdp", ("rep", "tp")),
        P("fsdp", ("rep", "tp")),
        P(),
        P(("rep", "fsdp", "tp"), None),
        P(None, ("rep", "fsdp", "tp"), None),
        P(None, ("rep", "fsdp", "tp"), None, None),
        P(("rep", "fsdp", "tp"), None, None, None),
        P(("rep", "fsdp", "tp"), None),
        P(("rep", "fsdp", "tp")),
    )
    out_specs = P(("rep", "fsdp", "tp"), None)
    return jax.shard_map(shards, mesh=mesh, in_specs=in_specs, out_specs=out_specs, check_vma=False)
```

```python
import functools

import jax
import jax.numpy as jnp
from jax import lax
from jax.experimental import pallas as pl
from jax.experimental.pallas import tpu as pltpu
from jax.sharding import PartitionSpec as P

HD = 128
FULL_WIDTH = 4096
MESH = pl.DeviceIdType.MESH

beta_one = 0.9
beta_two = 0.95
adam_eps = 1e-08
adam_time = 100.0
norm_eps = 1e-05

TILE = 256
SUB = 128
SLOTS = 4
LAG = 3


def split_inputs(kv_pool, page_table, cache_len, new_kv):
    rows, per_row = page_table.shape
    pages, page, _, kv_width = kv_pool.shape
    keys = kv_pool[:, :, 0, :].reshape(pages * page, kv_width)
    values = kv_pool[:, :, 1, :].reshape(pages * page, kv_width)
    place = (jnp.arange(per_row, dtype=jnp.int32) * page)[None, :, None, None] + jnp.arange(
        page, dtype=jnp.int32
    )
    named = page_table[:, :, None] == jnp.arange(pages, dtype=jnp.int32)
    valid = named[..., None] & (place < cache_len[:, None, None, None])
    valid = jnp.any(valid, axis=1).reshape(rows, pages * page).astype(jnp.float32)
    fresh = new_kv.astype(jnp.float32).transpose(0, 2, 1, 3)
    return keys, values, valid, fresh


def block_kernel(
    n_rep,
    n_fsdp,
    n_tp,
    gu_master,
    gu_moment,
    gu_second,
    gu_grad,
    d_master,
    d_moment,
    d_second,
    d_grad,
    gain,
    start,
    queries,
    keys,
    values,
    valid,
    fresh,
    out,
    weights,
    slots,
    att,
    pieces,
    got_pieces,
    att_out,
    att_in,
    sums,
    x,
    own,
    core_out,
    core_in,
    y_out,
    y_in,
    hid,
    acc,
    down_out,
    down_in,
    squares,
    mixed,
    fin_out,
    fin_in,
    grad_sem,
    slot_sem,
    f_send,
    f_recv,
    a_send,
    a_recv,
    s_send,
    s_recv,
    x_send,
    x_recv,
    core_send,
    core_recv,
    y_send,
    y_recv,
    h_send,
    h_recv,
    hc_send,
    hc_recv,
    d_send,
    d_recv,
):
    n_group = n_rep * n_tp
    members = n_fsdp // 2
    depth, cols = d_grad.shape
    tiles = cols // TILE
    steps = queries.shape[0]
    width = n_fsdp * depth
    units = 3 * tiles
    half = x.shape[1] * x.shape[2]
    part = half // members

    r = lax.axis_index("rep")
    f = lax.axis_index("fsdp")
    t = lax.axis_index("tp")
    g = r * n_tp + t
    c = lax.rem(f, 2)
    m = f // 2

    def f_dev(k):
        return (r, lax.rem(f + k, n_fsdp), t)

    def g_dev(k):
        there = lax.rem(g + k, n_group)
        return (there // n_tp, f, lax.rem(there, n_tp))

    def m_dev(k):
        return (r, lax.rem(m + k, members) * 2 + c, t)

    sibling = (r, m * 2 + 1 - c, t)

    barrier = pltpu.get_barrier_semaphore()
    for k in range(1, n_fsdp):
        pl.semaphore_signal(barrier, inc=1, device_id=f_dev(k), device_id_type=MESH)
    for k in range(1, n_group):
        pl.semaphore_signal(barrier, inc=1, device_id=g_dev(k), device_id_type=MESH)

    def tile_of(j):
        return pl.ds(pl.multiple_of(j * TILE, TILE), TILE)

    def grad_copies(j):
        at = tile_of(j)
        return [
            pltpu.make_async_copy(gu_grad.at[0, :, at], weights.at[0, j], grad_sem.at[0, j]),
            pltpu.make_async_copy(gu_grad.at[1, :, at], weights.at[1, j], grad_sem.at[1, j]),
            pltpu.make_async_copy(d_grad.at[:, at], weights.at[2, j], grad_sem.at[2, j]),
        ]

    def pair_copies(a, j):
        slot = lax.rem(2 * j + a, SLOTS)
        return [
            pltpu.make_async_copy(ref.at[a, :, tile_of(j)], slots.at[slot, i], slot_sem.at[slot, i])
            for i, ref in enumerate((gu_master, gu_moment, gu_second))
        ]

    def down_copies(j):
        slot = lax.rem(2 * tiles + j, SLOTS)
        return [
            pltpu.make_async_copy(ref.at[:, tile_of(j)], slots.at[slot, i], slot_sem.at[slot, i])
            for i, ref in enumerate((d_master, d_moment, d_second))
        ]

    def start_all(copies):
        for copy in copies:
            copy.start()

    def wait_all(copies):
        for copy in copies:
            copy.wait()

    def start_grads(j, carry):
        start_all(grad_copies(j))
        return carry

    lax.fori_loop(0, tiles, start_grads, 0)
    for n in range(SLOTS):
        start_all(pair_copies(n % 2, n // 2))

    pl.semaphore_wait(barrier, n_fsdp + n_group - 2)

    def remote(src, dst, send, recv, dev):
        return pltpu.make_async_remote_copy(
            src_ref=src, dst_ref=dst, send_sem=send, recv_sem=recv, device_id=dev, device_id_type=MESH
        )

    def squares_of(j, run):
        wait_all(grad_copies(j))
        for a in range(3):

            def square(b, run, a=a):
                v = weights[a, j, pl.ds(pl.multiple_of(b * SUB, SUB), SUB), :].astype(jnp.float32)
                return run + jnp.sum((v * v).reshape(SUB // 8, 8, TILE), axis=0)

            run = lax.fori_loop(0, depth // SUB, square, run)
        return run

    total = lax.fori_loop(0, tiles, squares_of, jnp.zeros((8, TILE), jnp.float32))
    tile_sum = total[:, :128]
    for b in range(1, TILE // 128):
        tile_sum = tile_sum + total[:, b * 128 : (b + 1) * 128]

    def send_sums(value, base, n, dev):
        sums[base] = value
        copies = [
            remote(sums.at[base], sums.at[base + k], s_send.at[base + k], s_recv.at[base + k], dev(k))
            for k in range(1, n)
        ]
        start_all(copies)
        return copies

    def add_sums(copies, value, base, n):
        wait_all(copies)
        for k in range(1, n):
            value = value + sums[base + k]
        return value

    def attend(step):
        heads = keys.shape[1] // HD
        group = width // keys.shape[1]
        scale = HD**-0.5
        mask = jnp.concatenate([valid[...]] * group, axis=0) > 0.5
        query = queries[step].astype(jnp.float32)
        for j in range(heads):
            lanes = slice(j * HD, (j + 1) * HD)
            q = jnp.concatenate(
                [query[:, (j * group + i) * HD : (j * group + i + 1) * HD] for i in range(group)], axis=0
            )
            old = lax.dot_general(
                q.astype(jnp.bfloat16),
                keys[:, lanes],
                (((1,), (1,)), ((), ())),
                preferred_element_type=jnp.float32,
            )
            old = jnp.where(mask, old * scale, -1e30)
            top = jnp.max(old, axis=1, keepdims=True)
            new = []
            for n in range(step + 1):
                k = jnp.concatenate([fresh[n, 0, :, lanes]] * group, axis=0)
                new.append(jnp.sum(q * k, axis=1, keepdims=True) * scale)
                top = jnp.maximum(top, new[n])
            old = jnp.exp(old - top)
            new = [jnp.exp(e - top) for e in new]
            whole = jnp.sum(old, axis=1, keepdims=True)
            for e in new:
                whole = whole + e
            y = jnp.dot(
                (old / whole).astype(jnp.bfloat16), values[:, lanes], preferred_element_type=jnp.float32
            )
            for n in range(step + 1):
                v = jnp.concatenate([fresh[n, 1, :, lanes]] * group, axis=0)
                y = y + (new[n] / whole).astype(jnp.bfloat16).astype(jnp.float32) * v
            for i in range(group):
                at = j * group + i
                att[:, at * HD : (at + 1) * HD] = y[i * 8 : (i + 1) * 8, :]

    sum_copies = send_sums(tile_sum, 0, n_fsdp, f_dev)
    attend(0)
    tile_sum = add_sums(sum_copies, tile_sum, 0, n_fsdp)
    sum_copies = send_sums(tile_sum, n_fsdp, n_group, g_dev)

    blend = (start[...].astype(jnp.float32) + att[...]).astype(jnp.bfloat16).astype(jnp.float32)
    factor = lax.rsqrt(jnp.sum(blend * blend, axis=1, keepdims=True) / width + norm_eps)
    for k in range(n_fsdp):
        cut = blend[:, k * depth : (k + 1) * depth]
        pieces[k, :8, :] = cut * factor * gain[k]
        pieces[k, 8:, :] = cut
    piece_copies = []
    for k in range(1, n_fsdp):
        there = lax.rem(f + k, n_fsdp)
        piece_copies.append(
            remote(pieces.at[there], got_pieces.at[k], f_send.at[k], f_recv.at[k], f_dev(k))
        )
    start_all(piece_copies)
    got_pieces[0] = pieces[f]
    wait_all(piece_copies)

    def joined(ref, a):
        at = pl.ds(a * 8, 8)
        blocks = [ref[lax.rem(f - b + n_fsdp, n_fsdp), at, :] for b in range(n_fsdp)]
        return jnp.concatenate(blocks, axis=0)

    x[0, 0] = joined(got_pieces, 0).astype(jnp.bfloat16)
    mixed[...] = joined(got_pieces, 1)

    def x_copies():
        return [
            remote(
                x.at[0, 0], x.at[k // x.shape[1], k % x.shape[1]], x_send.at[k], x_recv.at[k], g_dev(k)
            )
            for k in range(1, n_group)
        ]

    start_all(x_copies())
    tile_sum = add_sums(sum_copies, tile_sum, n_fsdp, n_group)
    clip = jnp.minimum(1.0, lax.rsqrt(jnp.sum(tile_sum, keepdims=True)))

    rate = 2.0 / FULL_WIDTH**0.5 / (1.0 - beta_one**adam_time)
    keep_m = rate * beta_one
    add_m = rate * (1.0 - beta_one)
    second_fix = 1.0 - beta_two**adam_time
    keep_v = beta_two / second_fix
    add_v = (1.0 - beta_two) / second_fix

    def update(s, j, slot):
        def rows_at(b, carry):
            at = pl.ds(pl.multiple_of(b * SUB, SUB), SUB)
            grad = weights[s, j, at, :].astype(jnp.float32) * clip
            first = keep_m * slots[slot, 1, at, :] + add_m * grad
            second = keep_v * slots[slot, 2, at, :] + add_v * (grad * grad)
            new = slots[slot, 0, at, :] - first / (jnp.sqrt(second) + adam_eps)
            weights[s, j, at, :] = new.astype(jnp.bfloat16)
            return carry

        lax.fori_loop(0, depth // SUB, rows_at, 0)


    def core_copy(j):
        return remote(core_out.at[j], core_in.at[j], core_send.at[j], core_recv.at[j], sibling)

    def y_copy(j, k):
        there = lax.rem(m + k, members)
        return remote(
            y_out.at[j, there], y_in.at[j, k - 1], y_send.at[j, k - 1], y_recv.at[j, k - 1], m_dev(k)
        )

    def h_copy(j, k):
        return remote(
            hid.at[j, c, m], hid.at[j, c, m], h_send.at[j, k - 1], h_recv.at[j, k - 1], m_dev(k)
        )

    def h_arrival(j, k):
        there = lax.rem(m - k + members, members)
        return remote(
            hid.at[j, c, m], hid.at[j, c, there], h_send.at[j, k - 1], h_recv.at[j, k - 1], m_dev(k)
        )

    def hc_copy(j):
        return remote(hid.at[j, c], hid.at[j, c], hc_send.at[j], hc_recv.at[j], sibling)

    def hc_arrival(j):
        return remote(hid.at[j, c], hid.at[j, 1 - c], hc_send.at[j], hc_recv.at[j], sibling)

    def multiply(j):
        theirs = x[1 - c].reshape(half, depth)
        mine = x[c].reshape(half, depth)
        both = jnp.concatenate([theirs, mine], axis=0)
        for a in range(2):
            y = jnp.dot(both, weights[a, j], preferred_element_type=jnp.float32)
            core_out[j, :, a * TILE : (a + 1) * TILE] = y[:half].astype(jnp.bfloat16)
            own[j, :, a * TILE : (a + 1) * TILE] = y[half:]
        core_copy(j).start()

    def add_core(j):
        core_copy(j).wait()
        y = own[j] + core_in[j].astype(jnp.float32)
        own[j] = y
        y_out[j] = y.astype(jnp.bfloat16).reshape(members, part, 2 * TILE)
        for k in range(1, members):
            y_copy(j, k).start()

    def second_stage(j):
        y = own[j, pl.ds(pl.multiple_of(m * part, part), part), :]
        for k in range(1, members):
            y_copy(j, k).wait()
            y = y + y_in[j, k - 1].astype(jnp.float32)
        gate, upper = y[:, :TILE], y[:, TILE:]
        hid[j, c, m] = (gate * jax.nn.sigmoid(gate) * upper).astype(jnp.bfloat16)
        for k in range(1, members):
            h_copy(j, k).start()

    def third_stage(j):
        for k in range(1, members):
            h_copy(j, k).wait_send()
            h_arrival(j, k).wait_recv()
        hc_copy(j).start()

    def fourth_stage(j):
        hc_copy(j).wait_send()
        hc_arrival(j).wait_recv()
        acc[...] += lax.dot_general(
            hid[j].reshape(2 * half, TILE),
            weights[2, j],
            (((1,), (1,)), ((), ())),
            preferred_element_type=jnp.float32,
        )

    def after(j, first, stage):
        @pl.when(first <= j)
        def _():
            stage(j - first)

    def before(j, first, stage):
        @pl.when(j < tiles - first)
        def _():
            stage(j + first)

    def update_pair(j, carry):
        for a in range(2):
            wait_all(pair_copies(a, j))
            update(a, j, lax.rem(2 * j + a, SLOTS))

            @pl.when(j + SLOTS // 2 < tiles)
            def _():
                start_all(pair_copies(a, j + SLOTS // 2))

            @pl.when(j + SLOTS // 2 >= tiles)
            def _():
                start_all(down_copies(2 * (j + SLOTS // 2 - tiles) + a))

        @pl.when(j == LAG)
        def _():
            wait_all(x_copies())

        after(j, LAG, multiply)
        after(j, LAG + 1, add_core)
        after(j, LAG + 2, second_stage)
        after(j, LAG + 3, third_stage)
        return carry

    def update_down(j, carry):
        wait_all(down_copies(j))
        update(2, j, lax.rem(2 * tiles + j, SLOTS))

        @pl.when(j + SLOTS < tiles)
        def _():
            start_all(down_copies(j + SLOTS))

        before(j, tiles - LAG, multiply)
        before(j, tiles - LAG - 1, add_core)
        before(j, tiles - LAG - 2, second_stage)
        before(j, tiles - LAG - 3, third_stage)
        after(j, 2, fourth_stage)
        return carry

    def looped(stage, first, last):
        def body(j, carry):
            stage(j)
            return carry

        lax.fori_loop(first, last, body, 0)

    for step in range(steps):
        acc[...] = jnp.zeros_like(acc)
        if step == 0:
            lax.fori_loop(0, tiles, update_pair, 0)
            lax.fori_loop(0, tiles, update_down, 0)
            looped(fourth_stage, tiles - 2, tiles)
        else:

            def first_stage(j):
                multiply(j)
                after(j, 1, add_core)

            looped(first_stage, 0, tiles)
            add_core(tiles - 1)
            looped(second_stage, 0, tiles)
            looped(third_stage, 0, tiles)
            looped(fourth_stage, 0, tiles)

        rows_of = acc.shape[0] // n_group
        copies = []
        for k in range(1, n_group):
            down_out[k] = acc[k * rows_of : (k + 1) * rows_of, :].astype(jnp.bfloat16)
            copy = remote(
                down_out.at[k], down_in.at[k], d_send.at[k], d_recv.at[k], g_dev(n_group - k)
            )
            copy.start()
            copies.append(copy)
        if step < steps - 1:
            attend(step + 1)
            for k in range(n_fsdp):
                att_out[k] = att[:, k * depth : (k + 1) * depth]
            att_copies = [
                remote(
                    att_out.at[lax.rem(f + k, n_fsdp)], att_in.at[k], a_send.at[k], a_recv.at[k], f_dev(k)
                )
                for k in range(1, n_fsdp)
            ]
            start_all(att_copies)
            att_in[0] = att_out[f]
            wait_all(att_copies)
        summed = acc[:rows_of, :]
        for k in range(1, n_group):
            copies[k - 1].wait()
            summed = summed + down_in[k].astype(jnp.float32)
        rows = (mixed[...] + summed).astype(jnp.bfloat16).astype(jnp.float32)

        if step < steps - 1:
            blend = (rows + joined(att_in, 0)).astype(jnp.bfloat16).astype(jnp.float32)
            mixed[...] = blend
            local = jnp.sum(blend * blend, axis=1, keepdims=True)
            squares[0] = jnp.broadcast_to(local, squares.shape[1:])
            copies = []
            for k in range(1, n_fsdp):
                copy = remote(squares.at[0], squares.at[k], f_send.at[k], f_recv.at[k], f_dev(k))
                copy.start()
                copies.append(copy)
            for copy in copies:
                copy.wait()
            whole = squares[0]
            for k in range(1, n_fsdp):
                whole = whole + squares[k]
            factor = lax.rsqrt(whole[:, :1] / (depth * n_fsdp) + norm_eps)
            x[0, 0] = (mixed[...] * factor * gain[f]).astype(jnp.bfloat16)
            start_all(x_copies())
            wait_all(x_copies())
        else:
            for k in range(n_fsdp):
                fin_out[k] = rows[k * 8 : (k + 1) * 8, :]
            copies = []
            for k in range(1, n_fsdp):
                there = lax.rem(f + k, n_fsdp)
                copy = remote(fin_out.at[there], fin_in.at[k], f_send.at[k], f_recv.at[k], f_dev(k))
                copy.start()
                copies.append(copy)
            out[f] = fin_out[f]
            for k in range(1, n_fsdp):
                copies[k - 1].wait()
                out[lax.rem(f - k + n_fsdp, n_fsdp)] = fin_in[k]


def shards(
    gate_up_master,
    gate_up_moment,
    gate_up_second,
    gate_up_grad,
    down_master,
    down_moment,
    down_second,
    down_grad,
    norm_gain,
    start_rows,
    queries,
    new_kv,
    kv_pool,
    page_table,
    cache_len,
):
    n_rep, n_fsdp, n_tp = (lax.axis_size(a) for a in ("rep", "fsdp", "tp"))
    n_group = n_rep * n_tp
    depth, cols = down_grad.shape
    local_rows, width = start_rows.shape
    steps = queries.shape[0]
    tiles = cols // TILE
    members = n_fsdp // 2
    block = local_rows * n_fsdp
    all_rows = block * n_group
    half = all_rows // 2

    keys, values, valid, fresh = split_inputs(kv_pool, page_table, cache_len, new_kv)
    gain = norm_gain.reshape(n_fsdp, 1, depth)

    bf16, f32 = jnp.bfloat16, jnp.float32
    dma = pltpu.SemaphoreType.DMA
    final = pl.pallas_call(
        functools.partial(block_kernel, n_rep, n_fsdp, n_tp),
        out_shape=jax.ShapeDtypeStruct((n_fsdp, local_rows, depth), f32),
        in_specs=[pl.BlockSpec(memory_space=pl.ANY)] * 8 + [pl.BlockSpec(memory_space=pltpu.VMEM)] * 7,
        out_specs=pl.BlockSpec(memory_space=pltpu.VMEM),
        scratch_shapes=[
            pltpu.VMEM((3, tiles, depth, TILE), bf16),
            pltpu.VMEM((SLOTS, 3, depth, TILE), f32),
            pltpu.VMEM((local_rows, width), f32),
            pltpu.VMEM((n_fsdp, 2 * local_rows, depth), f32),
            pltpu.VMEM((n_fsdp, 2 * local_rows, depth), f32),
            pltpu.VMEM((n_fsdp, local_rows, depth), f32),
            pltpu.VMEM((n_fsdp, local_rows, depth), f32),
            pltpu.VMEM((n_fsdp + n_group, 8, 128), f32),
            pltpu.VMEM((2, n_group // 2, block, depth), bf16),
            pltpu.VMEM((tiles, half, 2 * TILE), f32),
            pltpu.VMEM((tiles, half, 2 * TILE), bf16),
            pltpu.VMEM((tiles, half, 2 * TILE), bf16),
            pltpu.VMEM((tiles, members, half // members, 2 * TILE), bf16),
            pltpu.VMEM((tiles, members - 1, half // members, 2 * TILE), bf16),
            pltpu.VMEM((tiles, 2, members, half // members, TILE), bf16),
            pltpu.VMEM((all_rows, depth), f32),
            pltpu.VMEM((n_group, block, depth), bf16),
            pltpu.VMEM((n_group, block, depth), bf16),
            pltpu.VMEM((n_fsdp, block, 128), f32),
            pltpu.VMEM((block, depth), f32),
            pltpu.VMEM((n_fsdp, local_rows, depth), f32),
            pltpu.VMEM((n_fsdp, local_rows, depth), f32),
            dma((3, tiles)),
            dma((SLOTS, 3)),
            dma((n_fsdp,)),
            dma((n_fsdp,)),
            dma((n_fsdp,)),
            dma((n_fsdp,)),
            dma((n_fsdp + n_group,)),
            dma((n_fsdp + n_group,)),
            dma((n_group,)),
            dma((n_group,)),
            dma((tiles,)),
            dma((tiles,)),
            dma((tiles, members - 1)),
            dma((tiles, members - 1)),
            dma((tiles, members - 1)),
            dma((tiles, members - 1)),
            dma((tiles,)),
            dma((tiles,)),
            dma((n_group,)),
            dma((n_group,)),
        ],
        compiler_params=pltpu.CompilerParams(
            collective_id=0, has_side_effects=True, vmem_limit_bytes=60 * 2**20
        ),
        cost_estimate=pl.CostEstimate(
            flops=2 * steps * all_rows * 3 * depth * cols,
            bytes_accessed=3 * depth * cols * 14,
            transcendentals=3 * depth * cols,
        ),
        name="update_and_decode",
    )(
        gate_up_master,
        gate_up_moment,
        gate_up_second,
        gate_up_grad,
        down_master,
        down_moment,
        down_second,
        down_grad,
        gain,
        start_rows,
        queries,
        keys,
        values,
        valid,
        fresh,
    )
    return final.transpose(1, 0, 2).reshape(local_rows, width).astype(jnp.bfloat16)


def solution(mesh):
    in_specs = (
        P(None, "fsdp", ("rep", "tp")),
        P(None, "fsdp", ("rep", "tp")),
        P(None, "fsdp", ("rep", "tp")),
        P(None, "fsdp", ("rep", "tp")),
        P("fsdp", ("rep", "tp")),
        P("fsdp", ("rep", "tp")),
        P("fsdp", ("rep", "tp")),
        P("fsdp", ("rep", "tp")),
        P(),
        P(("rep", "fsdp", "tp"), None),
        P(None, ("rep", "fsdp", "tp"), None),
        P(None, ("rep", "fsdp", "tp"), None, None),
        P(("rep", "fsdp", "tp"), None, None, None),
        P(("rep", "fsdp", "tp"), None),
        P(("rep", "fsdp", "tp")),
    )
    out_specs = P(("rep", "fsdp", "tp"), None)
    return jax.shard_map(shards, mesh=mesh, in_specs=in_specs, out_specs=out_specs, check_vma=False)
```

```python
import functools

import jax
import jax.numpy as jnp
from jax import lax
from jax.experimental import pallas as pl
from jax.experimental.pallas import tpu as pltpu
from jax.sharding import PartitionSpec as P

HD = 128
FULL_WIDTH = 4096
MESH = pl.DeviceIdType.MESH

beta_one = 0.9
beta_two = 0.95
adam_eps = 1e-08
adam_time = 100.0
norm_eps = 1e-05

TILE = 256
SUB = 32
SQUARES = 128
SLOTS = 4
LAG = 3


def block_kernel(
    n_rep,
    n_fsdp,
    n_tp,
    page,
    gu_master,
    gu_moment,
    gu_second,
    gu_grad,
    d_master,
    d_moment,
    d_second,
    d_grad,
    gain,
    start,
    queries,
    kv_raw,
    table,
    length,
    fresh,
    out,
    weights,
    slots,
    kv,
    valid,
    att,
    pieces,
    got_pieces,
    att_out,
    att_in,
    sums,
    x,
    own,
    core_out,
    core_in,
    y_out,
    y_in,
    hid,
    acc,
    down_out,
    down_in,
    squares,
    mixed,
    fin_out,
    fin_in,
    grad_sem,
    slot_sem,
    f_send,
    f_recv,
    a_send,
    a_recv,
    s_send,
    s_recv,
    x_send,
    x_recv,
    core_send,
    core_recv,
    y_send,
    y_recv,
    h_send,
    h_recv,
    hc_send,
    hc_recv,
    d_send,
    d_recv,
):
    n_group = n_rep * n_tp
    members = n_fsdp // 2
    depth, cols = d_grad.shape
    tiles = cols // TILE
    steps = queries.shape[0]
    width = n_fsdp * depth
    units = 3 * tiles
    half = x.shape[1] * x.shape[2]
    part = half // members

    r = lax.axis_index("rep")
    f = lax.axis_index("fsdp")
    t = lax.axis_index("tp")
    g = r * n_tp + t
    c = lax.rem(f, 2)
    m = f // 2

    def f_dev(k):
        return (r, lax.rem(f + k, n_fsdp), t)

    def g_dev(k):
        there = lax.rem(g + k, n_group)
        return (there // n_tp, f, lax.rem(there, n_tp))

    def z_dev(k):
        return (r, f, lax.rem(t + k, n_tp))

    def r_dev(k):
        return (lax.rem(r + k, n_rep), f, t)

    def m_dev(k):
        return (r, lax.rem(m + k, members) * 2 + c, t)

    sibling = (r, m * 2 + 1 - c, t)

    barrier = pltpu.get_barrier_semaphore()
    for k in range(1, n_fsdp):
        pl.semaphore_signal(barrier, inc=1, device_id=f_dev(k), device_id_type=MESH)
    for k in range(1, n_group):
        pl.semaphore_signal(barrier, inc=1, device_id=g_dev(k), device_id_type=MESH)

    def tile_of(j):
        return pl.ds(pl.multiple_of(j * TILE, TILE), TILE)

    def grad_copies(j):
        at = tile_of(j)
        return [
            pltpu.make_async_copy(gu_grad.at[0, :, at], weights.at[0, j], grad_sem.at[0, j]),
            pltpu.make_async_copy(gu_grad.at[1, :, at], weights.at[1, j], grad_sem.at[1, j]),
            pltpu.make_async_copy(d_grad.at[:, at], weights.at[2, j], grad_sem.at[2, j]),
        ]

    def pair_copies(a, j):
        slot = lax.rem(2 * j + a, SLOTS)
        return [
            pltpu.make_async_copy(ref.at[a, :, tile_of(j)], slots.at[slot, i], slot_sem.at[slot, i])
            for i, ref in enumerate((gu_master, gu_moment, gu_second))
        ]

    def down_copies(j):
        slot = lax.rem(2 * tiles + j, SLOTS)
        return [
            pltpu.make_async_copy(ref.at[:, tile_of(j)], slots.at[slot, i], slot_sem.at[slot, i])
            for i, ref in enumerate((d_master, d_moment, d_second))
        ]

    def start_all(copies):
        for copy in copies:
            copy.start()

    def wait_all(copies):
        for copy in copies:
            copy.wait()

    def start_grads(j, carry):
        start_all(grad_copies(j))
        return carry

    lax.fori_loop(0, tiles, start_grads, 0)
    for n in range(SLOTS):
        start_all(pair_copies(n % 2, n // 2))

    pl.semaphore_wait(barrier, n_fsdp + n_group - 2)

    def remote(src, dst, send, recv, dev):
        return pltpu.make_async_remote_copy(
            src_ref=src, dst_ref=dst, send_sem=send, recv_sem=recv, device_id=dev, device_id_type=MESH
        )

    def squares_of(j, run):
        wait_all(grad_copies(j))
        for a in range(3):

            def square(b, run, a=a):
                v = weights[a, j, pl.ds(pl.multiple_of(b * SQUARES, SQUARES), SQUARES), :]
                v = v.astype(jnp.float32)
                return run + jnp.sum((v * v).reshape(SQUARES // 8, 8, TILE), axis=0)

            run = lax.fori_loop(0, depth // SQUARES, square, run)
        return run

    total = lax.fori_loop(0, tiles, squares_of, jnp.zeros((8, TILE), jnp.float32))
    tile_sum = total[:, :128]
    for b in range(1, TILE // 128):
        tile_sum = tile_sum + total[:, b * 128 : (b + 1) * 128]

    def send_sums(value, base, n, dev):
        sums[base] = value
        copies = [
            remote(sums.at[base], sums.at[base + k], s_send.at[base + k], s_recv.at[base + k], dev(k))
            for k in range(1, n)
        ]
        start_all(copies)
        return copies

    def add_sums(copies, value, base, n):
        wait_all(copies)
        for k in range(1, n):
            value = value + sums[base + k]
        return value

    def unpage(b, carry):
        at = pl.ds(pl.multiple_of(b * 2 * page, 2 * page), 2 * page)
        kv[at, :] = kv_raw[b].reshape(2 * page, kv.shape[1])
        return carry

    lax.fori_loop(0, kv_raw.shape[0], unpage, 0)

    lane = lax.broadcasted_iota(jnp.int32, valid.shape, 1)
    place = lax.rem(lane // 2, page)
    held = jnp.zeros(valid.shape, jnp.float32)
    for p in range(table.shape[1]):
        named = table[:, p : p + 1] == lane // (2 * page)
        held = jnp.where(named & (place + p * page < length[...]), 1.0, held)
    valid[...] = jnp.where(lax.rem(lane, 2) == 0, held, 0.0)

    heads = kv.shape[1] // HD
    group = width // kv.shape[1]

    def attend(step, first, last):
        scale = HD**-0.5
        mask = jnp.concatenate([valid[...]] * group, axis=0) > 0.5
        query = queries[step].astype(jnp.float32)
        for j in range(first, last):
            lanes = slice(j * HD, (j + 1) * HD)
            q = jnp.concatenate(
                [query[:, (j * group + i) * HD : (j * group + i + 1) * HD] for i in range(group)], axis=0
            )
            old = lax.dot_general(
                q.astype(jnp.bfloat16), kv[:, lanes], (((1,), (1,)), ((), ())), preferred_element_type=jnp.float32
            )
            old = jnp.where(mask, old * scale, -1e30)
            top = jnp.max(old, axis=1, keepdims=True)
            new = []
            for n in range(step + 1):
                k = jnp.concatenate([fresh[n, 0, :, lanes]] * group, axis=0)
                new.append(jnp.sum(q * k, axis=1, keepdims=True) * scale)
                top = jnp.maximum(top, new[n])
            old = jnp.exp(old - top)
            new = [jnp.exp(e - top) for e in new]
            whole = jnp.sum(old, axis=1, keepdims=True)
            for e in new:
                whole = whole + e
            inverse = 1.0 / whole
            prob = pltpu.roll(old * inverse, 1, 1).astype(jnp.bfloat16)
            y = jnp.dot(prob, kv[:, lanes], preferred_element_type=jnp.float32)
            for n in range(step + 1):
                v = jnp.concatenate([fresh[n, 1, :, lanes]] * group, axis=0)
                y = y + (new[n] * inverse).astype(jnp.bfloat16).astype(jnp.float32) * v
            for i in range(group):
                at = j * group + i
                att[:, at * HD : (at + 1) * HD] = y[i * 8 : (i + 1) * 8, :]

    sum_copies = send_sums(tile_sum, 0, n_fsdp, f_dev)
    attend(0, 0, heads)
    tile_sum = add_sums(sum_copies, tile_sum, 0, n_fsdp)
    sum_copies = send_sums(tile_sum, n_fsdp, n_group, g_dev)

    blend = (start[...].astype(jnp.float32) + att[...]).astype(jnp.bfloat16).astype(jnp.float32)
    factor = lax.rsqrt(jnp.sum(blend * blend, axis=1, keepdims=True) / width + norm_eps)
    for k in range(n_fsdp):
        cut = blend[:, k * depth : (k + 1) * depth]
        pieces[k, :8, :] = cut * factor * gain[k]
        pieces[k, 8:, :] = cut
    piece_copies = []
    for k in range(1, n_fsdp):
        there = lax.rem(f + k, n_fsdp)
        piece_copies.append(
            remote(pieces.at[there], got_pieces.at[k], f_send.at[k], f_recv.at[k], f_dev(k))
        )
    start_all(piece_copies)
    got_pieces[0] = pieces[f]
    wait_all(piece_copies)

    def joined(ref, a):
        at = pl.ds(a * 8, 8)
        blocks = [ref[lax.rem(f - b + n_fsdp, n_fsdp), at, :] for b in range(n_fsdp)]
        return jnp.concatenate(blocks, axis=0)

    x[0, 0] = joined(got_pieces, 0).astype(jnp.bfloat16)
    mixed[...] = joined(got_pieces, 1)

    def x_block(i):
        return x.at[i // x.shape[1], i % x.shape[1]]

    def x_along_tp():
        return [
            remote(x_block(0), x_block(k), x_send.at[k], x_recv.at[k], z_dev(k)) for k in range(1, n_tp)
        ]

    def x_along_rep(k):
        return [
            remote(x_block(k), x_block(i * n_tp + k), x_send.at[i * n_tp + k], x_recv.at[i * n_tp + k], r_dev(i))
            for i in range(1, n_rep)
        ]

    def x_start():
        start_all(x_along_tp())
        start_all(x_along_rep(0))

    def x_forward():
        for k, copy in enumerate(x_along_tp(), 1):
            copy.wait()
            start_all(x_along_rep(k))

    def x_finish():
        for k in range(n_tp):
            wait_all(x_along_rep(k))

    x_start()
    tile_sum = add_sums(sum_copies, tile_sum, n_fsdp, n_group)
    clip = jnp.minimum(1.0, lax.rsqrt(jnp.sum(tile_sum, keepdims=True)))

    rate = 2.0 / FULL_WIDTH**0.5 / (1.0 - beta_one**adam_time)
    keep_m = rate * beta_one
    add_m = rate * (1.0 - beta_one)
    second_fix = 1.0 - beta_two**adam_time
    keep_v = beta_two / second_fix
    add_v = (1.0 - beta_two) / second_fix

    clip_m = add_m * clip
    clip_v = add_v * clip * clip

    def update(s, j, slot):
        def rows_at(b, carry):
            at = pl.ds(pl.multiple_of(b * SUB, SUB), SUB)
            grad = weights[s, j, at, :].astype(jnp.float32)
            first = keep_m * slots[slot, 1, at, :] + clip_m * grad
            second = keep_v * slots[slot, 2, at, :] + clip_v * (grad * grad)
            under = second * lax.rsqrt(second) + adam_eps
            inverse = pl.reciprocal(under, approx=True)
            inverse = inverse * (2.0 - under * inverse)
            new = slots[slot, 0, at, :] - first * inverse
            weights[s, j, at, :] = new.astype(jnp.bfloat16)
            return carry

        lax.fori_loop(0, depth // SUB, rows_at, 0, unroll=2)


    def core_copy(j):
        return remote(core_out.at[j], core_in.at[j], core_send.at[j], core_recv.at[j], sibling)

    def y_copy(j, k):
        there = lax.rem(m + k, members)
        return remote(
            y_out.at[j, there], y_in.at[j, k - 1], y_send.at[j, k - 1], y_recv.at[j, k - 1], m_dev(k)
        )

    def h_copy(j, k):
        return remote(
            hid.at[j, c, m], hid.at[j, c, m], h_send.at[j, k - 1], h_recv.at[j, k - 1], m_dev(k)
        )

    def h_arrival(j, k):
        there = lax.rem(m - k + members, members)
        return remote(
            hid.at[j, c, m], hid.at[j, c, there], h_send.at[j, k - 1], h_recv.at[j, k - 1], m_dev(k)
        )

    def hc_copy(j):
        return remote(hid.at[j, c], hid.at[j, c], hc_send.at[j], hc_recv.at[j], sibling)

    def hc_arrival(j):
        return remote(hid.at[j, c], hid.at[j, 1 - c], hc_send.at[j], hc_recv.at[j], sibling)

    def multiply(j):
        theirs = x[1 - c].reshape(half, depth)
        mine = x[c].reshape(half, depth)
        both = jnp.concatenate([theirs, mine], axis=0)
        for a in range(2):
            y = jnp.dot(both, weights[a, j], preferred_element_type=jnp.float32)
            core_out[j, :, a * TILE : (a + 1) * TILE] = y[:half].astype(jnp.bfloat16)
            own[j, :, a * TILE : (a + 1) * TILE] = y[half:]
        core_copy(j).start()

    def add_core(j):
        core_copy(j).wait()
        y = own[j] + core_in[j].astype(jnp.float32)
        own[j] = y
        y_out[j] = y.astype(jnp.bfloat16).reshape(members, part, 2 * TILE)
        for k in range(1, members):
            y_copy(j, k).start()

    def second_stage(j):
        y = own[j, pl.ds(pl.multiple_of(m * part, part), part), :]
        for k in range(1, members):
            y_copy(j, k).wait()
            y = y + y_in[j, k - 1].astype(jnp.float32)
        gate, upper = y[:, :TILE], y[:, TILE:]
        hid[j, c, m] = (gate * jax.nn.sigmoid(gate) * upper).astype(jnp.bfloat16)
        for k in range(1, members):
            h_copy(j, k).start()

    def third_stage(j):
        for k in range(1, members):
            h_copy(j, k).wait_send()
            h_arrival(j, k).wait_recv()
        hc_copy(j).start()

    def fourth_stage(j):
        hc_copy(j).wait_send()
        hc_arrival(j).wait_recv()
        acc[...] += lax.dot_general(
            hid[j].reshape(2 * half, TILE),
            weights[2, j],
            (((1,), (1,)), ((), ())),
            preferred_element_type=jnp.float32,
        )

    def after(j, first, stage):
        @pl.when(first <= j)
        def _():
            stage(j - first)

    def before(j, first, stage):
        @pl.when(j < tiles - first)
        def _():
            stage(j + first)

    def update_pair(j, carry):
        for a in range(2):
            wait_all(pair_copies(a, j))
            update(a, j, lax.rem(2 * j + a, SLOTS))

            @pl.when(j + SLOTS // 2 < tiles)
            def _():
                start_all(pair_copies(a, j + SLOTS // 2))

            @pl.when(j + SLOTS // 2 >= tiles)
            def _():
                start_all(down_copies(2 * (j + SLOTS // 2 - tiles) + a))

        @pl.when(j == LAG - 2)
        def _():
            x_forward()

        @pl.when(j == LAG)
        def _():
            x_finish()

        after(j, LAG, multiply)
        after(j, LAG + 1, add_core)
        after(j, LAG + 2, second_stage)
        after(j, LAG + 3, third_stage)
        return carry

    def update_down(j, carry):
        wait_all(down_copies(j))
        update(2, j, lax.rem(2 * tiles + j, SLOTS))

        @pl.when(j + SLOTS < tiles)
        def _():
            start_all(down_copies(j + SLOTS))

        before(j, tiles - LAG, multiply)
        before(j, tiles - LAG - 1, add_core)
        before(j, tiles - LAG - 2, second_stage)
        before(j, tiles - LAG - 3, third_stage)
        after(j, 2, fourth_stage)
        return carry

    def looped(stage, first, last):
        def body(j, carry):
            stage(j)
            return carry

        lax.fori_loop(first, last, body, 0)

    for step in range(steps):
        acc[...] = jnp.zeros_like(acc)
        if step == 0:
            lax.fori_loop(0, tiles, update_pair, 0)
            lax.fori_loop(0, tiles, update_down, 0)
            looped(fourth_stage, tiles - 2, tiles)
        else:

            def first_stage(j):
                multiply(j)
                after(j, 1, add_core)

            looped(first_stage, 0, tiles)
            add_core(tiles - 1)
            looped(second_stage, 0, tiles)
            looped(third_stage, 0, tiles)
            looped(fourth_stage, 0, tiles)

        rows_of = acc.shape[0] // n_group

        def own_block(i):
            return acc[i * rows_of : (i + 1) * rows_of, :]

        def down_along_rep(k):
            return [
                remote(down_out.at[i], down_in.at[i], d_send.at[i], d_recv.at[i], r_dev(n_rep - i // n_tp))
                for i in range(n_tp + k, n_group, n_tp)
            ]

        def down_along_tp(k):
            return remote(down_out.at[k], down_in.at[k], d_send.at[k], d_recv.at[k], z_dev(n_tp - k))

        order = list(range(1, n_tp)) + [0]
        for k in order:
            for i in range(n_tp + k, n_group, n_tp):
                down_out[i] = own_block(i).astype(jnp.bfloat16)
            start_all(down_along_rep(k))
        summed = None
        done = 0
        for n, k in enumerate(order):
            if step < steps - 1:
                attend(step + 1, done, heads * (n + 1) // n_tp)
                done = heads * (n + 1) // n_tp
            wait_all(down_along_rep(k))
            summed = own_block(k)
            for i in range(n_tp + k, n_group, n_tp):
                summed = summed + down_in[i].astype(jnp.float32)
            if k > 0:
                down_out[k] = summed.astype(jnp.bfloat16)
                down_along_tp(k).start()
        if step < steps - 1:
            for k in range(n_fsdp):
                att_out[k] = att[:, k * depth : (k + 1) * depth]
            att_copies = [
                remote(
                    att_out.at[lax.rem(f + k, n_fsdp)], att_in.at[k], a_send.at[k], a_recv.at[k], f_dev(k)
                )
                for k in range(1, n_fsdp)
            ]
            start_all(att_copies)
            att_in[0] = att_out[f]
            wait_all(att_copies)
        for k in range(1, n_tp):
            down_along_tp(k).wait()
            summed = summed + down_in[k].astype(jnp.float32)
        rows = (mixed[...] + summed).astype(jnp.bfloat16).astype(jnp.float32)

        if step < steps - 1:
            blend = (rows + joined(att_in, 0)).astype(jnp.bfloat16).astype(jnp.float32)
            mixed[...] = blend
            local = jnp.sum(blend * blend, axis=1, keepdims=True)
            squares[0] = jnp.broadcast_to(local, squares.shape[1:])
            copies = []
            for k in range(1, n_fsdp):
                copy = remote(squares.at[0], squares.at[k], f_send.at[k], f_recv.at[k], f_dev(k))
                copy.start()
                copies.append(copy)
            for copy in copies:
                copy.wait()
            whole = squares[0]
            for k in range(1, n_fsdp):
                whole = whole + squares[k]
            factor = lax.rsqrt(whole[:, :1] / (depth * n_fsdp) + norm_eps)
            x[0, 0] = (mixed[...] * factor * gain[f]).astype(jnp.bfloat16)
            x_start()
            x_forward()
            x_finish()
        else:
            for k in range(n_fsdp):
                fin_out[k] = rows[k * 8 : (k + 1) * 8, :]
            copies = []
            for k in range(1, n_fsdp):
                there = lax.rem(f + k, n_fsdp)
                copy = remote(fin_out.at[there], fin_in.at[k], f_send.at[k], f_recv.at[k], f_dev(k))
                copy.start()
                copies.append(copy)
            out[f] = fin_out[f]
            for k in range(1, n_fsdp):
                copies[k - 1].wait()
                out[lax.rem(f - k + n_fsdp, n_fsdp)] = fin_in[k]


def shards(
    gate_up_master,
    gate_up_moment,
    gate_up_second,
    gate_up_grad,
    down_master,
    down_moment,
    down_second,
    down_grad,
    norm_gain,
    start_rows,
    queries,
    new_kv,
    kv_pool,
    page_table,
    cache_len,
):
    n_rep, n_fsdp, n_tp = (lax.axis_size(a) for a in ("rep", "fsdp", "tp"))
    n_group = n_rep * n_tp
    depth, cols = down_grad.shape
    local_rows, width = start_rows.shape
    steps = queries.shape[0]
    tiles = cols // TILE
    members = n_fsdp // 2
    block = local_rows * n_fsdp
    all_rows = block * n_group
    half = all_rows // 2

    pages, page, _, kv_width = kv_pool.shape
    kv = kv_pool
    fresh = new_kv.astype(jnp.float32).transpose(0, 2, 1, 3)
    gain = norm_gain.reshape(n_fsdp, 1, depth)

    bf16, f32 = jnp.bfloat16, jnp.float32
    dma = pltpu.SemaphoreType.DMA
    final = pl.pallas_call(
        functools.partial(block_kernel, n_rep, n_fsdp, n_tp, page),
        out_shape=jax.ShapeDtypeStruct((n_fsdp, local_rows, depth), f32),
        in_specs=[pl.BlockSpec(memory_space=pl.ANY)] * 8 + [pl.BlockSpec(memory_space=pltpu.VMEM)] * 7,
        out_specs=pl.BlockSpec(memory_space=pltpu.VMEM),
        scratch_shapes=[
            pltpu.VMEM((3, tiles, depth, TILE), bf16),
            pltpu.VMEM((SLOTS, 3, depth, TILE), f32),
            pltpu.VMEM((2 * pages * page, kv_width), bf16),
            pltpu.VMEM((local_rows, 2 * pages * page), f32),
            pltpu.VMEM((local_rows, width), f32),
            pltpu.VMEM((n_fsdp, 2 * local_rows, depth), f32),
            pltpu.VMEM((n_fsdp, 2 * local_rows, depth), f32),
            pltpu.VMEM((n_fsdp, local_rows, depth), f32),
            pltpu.VMEM((n_fsdp, local_rows, depth), f32),
            pltpu.VMEM((n_fsdp + n_group, 8, 128), f32),
            pltpu.VMEM((2, n_group // 2, block, depth), bf16),
            pltpu.VMEM((tiles, half, 2 * TILE), f32),
            pltpu.VMEM((tiles, half, 2 * TILE), bf16),
            pltpu.VMEM((tiles, half, 2 * TILE), bf16),
            pltpu.VMEM((tiles, members, half // members, 2 * TILE), bf16),
            pltpu.VMEM((tiles, members - 1, half // members, 2 * TILE), bf16),
            pltpu.VMEM((tiles, 2, members, half // members, TILE), bf16),
            pltpu.VMEM((all_rows, depth), f32),
            pltpu.VMEM((n_group, block, depth), bf16),
            pltpu.VMEM((n_group, block, depth), bf16),
            pltpu.VMEM((n_fsdp, block, 128), f32),
            pltpu.VMEM((block, depth), f32),
            pltpu.VMEM((n_fsdp, local_rows, depth), f32),
            pltpu.VMEM((n_fsdp, local_rows, depth), f32),
            dma((3, tiles)),
            dma((SLOTS, 3)),
            dma((n_fsdp,)),
            dma((n_fsdp,)),
            dma((n_fsdp,)),
            dma((n_fsdp,)),
            dma((n_fsdp + n_group,)),
            dma((n_fsdp + n_group,)),
            dma((n_group,)),
            dma((n_group,)),
            dma((tiles,)),
            dma((tiles,)),
            dma((tiles, members - 1)),
            dma((tiles, members - 1)),
            dma((tiles, members - 1)),
            dma((tiles, members - 1)),
            dma((tiles,)),
            dma((tiles,)),
            dma((n_group,)),
            dma((n_group,)),
        ],
        compiler_params=pltpu.CompilerParams(
            collective_id=0, has_side_effects=True, vmem_limit_bytes=60 * 2**20
        ),
        cost_estimate=pl.CostEstimate(
            flops=2 * steps * all_rows * 3 * depth * cols,
            bytes_accessed=3 * depth * cols * 14,
            transcendentals=3 * depth * cols,
        ),
        name="update_and_decode",
    )(
        gate_up_master,
        gate_up_moment,
        gate_up_second,
        gate_up_grad,
        down_master,
        down_moment,
        down_second,
        down_grad,
        gain,
        start_rows,
        queries,
        kv,
        page_table,
        cache_len.reshape(local_rows, 1),
        fresh,
    )
    return final.transpose(1, 0, 2).reshape(local_rows, width).astype(jnp.bfloat16)


def solution(mesh):
    in_specs = (
        P(None, "fsdp", ("rep", "tp")),
        P(None, "fsdp", ("rep", "tp")),
        P(None, "fsdp", ("rep", "tp")),
        P(None, "fsdp", ("rep", "tp")),
        P("fsdp", ("rep", "tp")),
        P("fsdp", ("rep", "tp")),
        P("fsdp", ("rep", "tp")),
        P("fsdp", ("rep", "tp")),
        P(),
        P(("rep", "fsdp", "tp"), None),
        P(None, ("rep", "fsdp", "tp"), None),
        P(None, ("rep", "fsdp", "tp"), None, None),
        P(("rep", "fsdp", "tp"), None, None, None),
        P(("rep", "fsdp", "tp"), None),
        P(("rep", "fsdp", "tp")),
    )
    out_specs = P(("rep", "fsdp", "tp"), None)
    return jax.shard_map(shards, mesh=mesh, in_specs=in_specs, out_specs=out_specs, check_vma=False)
```

```python
import functools

import jax
import jax.numpy as jnp
from jax import lax
from jax.experimental import pallas as pl
from jax.experimental.pallas import tpu as pltpu
from jax.sharding import PartitionSpec as P

HD = 128
FULL_WIDTH = 4096
MESH = pl.DeviceIdType.MESH

beta_one = 0.9
beta_two = 0.95
adam_eps = 1e-08
adam_time = 100.0
norm_eps = 1e-05

TILE = 256
SUB = 32
SQUARES = 128
SLOTS = 4
LAG = 4


def block_kernel(
    n_rep,
    n_fsdp,
    n_tp,
    page,
    gu_master,
    gu_moment,
    gu_second,
    gu_grad,
    d_master,
    d_moment,
    d_second,
    d_grad,
    gain,
    start,
    queries,
    kv_raw,
    table,
    length,
    fresh,
    out,
    weights,
    slots,
    kv,
    valid,
    att,
    pieces,
    got_pieces,
    sums,
    x,
    own,
    core_out,
    core_in,
    y_out,
    y_in,
    hid,
    acc,
    down_out,
    down_in,
    squares,
    mixed,
    fin_out,
    fin_in,
    grad_sem,
    slot_sem,
    f_send,
    f_recv,
    s_send,
    s_recv,
    x_send,
    x_recv,
    core_send,
    core_recv,
    y_send,
    y_recv,
    h_send,
    h_recv,
    hc_send,
    hc_recv,
    d_send,
    d_recv,
):
    n_group = n_rep * n_tp
    members = n_fsdp // 2
    depth, cols = d_grad.shape
    tiles = cols // TILE
    steps = queries.shape[0]
    width = n_fsdp * depth
    units = 3 * tiles
    half = x.shape[1] * x.shape[2]
    part = half // members

    r = lax.axis_index("rep")
    f = lax.axis_index("fsdp")
    t = lax.axis_index("tp")
    g = r * n_tp + t
    c = lax.rem(f, 2)
    m = f // 2

    def f_dev(k):
        return (r, lax.rem(f + k, n_fsdp), t)

    def g_dev(k):
        there = lax.rem(g + k, n_group)
        return (there // n_tp, f, lax.rem(there, n_tp))

    def z_dev(k):
        return (r, f, lax.rem(t + k, n_tp))

    def r_dev(k):
        return (lax.rem(r + k, n_rep), f, t)

    def m_dev(k):
        return (r, lax.rem(m + k, members) * 2 + c, t)

    sibling = (r, m * 2 + 1 - c, t)

    barrier = pltpu.get_barrier_semaphore()
    for k in range(1, n_fsdp):
        pl.semaphore_signal(barrier, inc=1, device_id=f_dev(k), device_id_type=MESH)
    for k in range(1, n_group):
        pl.semaphore_signal(barrier, inc=1, device_id=g_dev(k), device_id_type=MESH)

    def tile_of(j):
        return pl.ds(pl.multiple_of(j * TILE, TILE), TILE)

    def grad_copies(j):
        at = tile_of(j)
        return [
            pltpu.make_async_copy(gu_grad.at[0, :, at], weights.at[0, j], grad_sem.at[0, j]),
            pltpu.make_async_copy(gu_grad.at[1, :, at], weights.at[1, j], grad_sem.at[1, j]),
            pltpu.make_async_copy(d_grad.at[:, at], weights.at[2, j], grad_sem.at[2, j]),
        ]

    def pair_copies(a, j):
        slot = lax.rem(2 * j + a, SLOTS)
        return [
            pltpu.make_async_copy(ref.at[a, :, tile_of(j)], slots.at[slot, i], slot_sem.at[slot, i])
            for i, ref in enumerate((gu_master, gu_moment, gu_second))
        ]

    def down_copies(j):
        slot = lax.rem(2 * tiles + j, SLOTS)
        return [
            pltpu.make_async_copy(ref.at[:, tile_of(j)], slots.at[slot, i], slot_sem.at[slot, i])
            for i, ref in enumerate((d_master, d_moment, d_second))
        ]

    def start_all(copies):
        for copy in copies:
            copy.start()

    def wait_all(copies):
        for copy in copies:
            copy.wait()

    def start_grads(j, carry):
        start_all(grad_copies(j))
        return carry

    lax.fori_loop(0, tiles, start_grads, 0)
    for n in range(SLOTS):
        start_all(pair_copies(n % 2, n // 2))

    pl.semaphore_wait(barrier, n_fsdp + n_group - 2)

    def remote(src, dst, send, recv, dev):
        return pltpu.make_async_remote_copy(
            src_ref=src, dst_ref=dst, send_sem=send, recv_sem=recv, device_id=dev, device_id_type=MESH
        )

    def unpage(b, carry):
        at = pl.ds(pl.multiple_of(b * 2 * page, 2 * page), 2 * page)
        kv[at, :] = kv_raw[b].reshape(2 * page, kv.shape[1])
        return carry

    lax.fori_loop(0, kv_raw.shape[0], unpage, 0)

    lane = lax.broadcasted_iota(jnp.int32, valid.shape, 1)
    place = lax.rem(lane // 2, page)
    held = jnp.zeros(valid.shape, jnp.float32)
    for p in range(table.shape[1]):
        named = table[:, p : p + 1] == lane // (2 * page)
        held = jnp.where(named & (place + p * page < length[...]), 1.0, held)
    valid[...] = jnp.where(lax.rem(lane, 2) == 0, held, 0.0)

    def squares_of(j, run):
        wait_all(grad_copies(j))
        for a in range(3):

            def square(b, run, a=a):
                v = weights[a, j, pl.ds(pl.multiple_of(b * SQUARES, SQUARES), SQUARES), :]
                v = v.astype(jnp.float32)
                return run + jnp.sum((v * v).reshape(SQUARES // 8, 8, TILE), axis=0)

            run = lax.fori_loop(0, depth // SQUARES, square, run)
        return run

    total = lax.fori_loop(0, tiles, squares_of, jnp.zeros((8, TILE), jnp.float32))
    tile_sum = total[:, :128]
    for b in range(1, TILE // 128):
        tile_sum = tile_sum + total[:, b * 128 : (b + 1) * 128]

    def send_sums(value, base, n, dev):
        sums[base] = value
        copies = [
            remote(sums.at[base], sums.at[base + k], s_send.at[base + k], s_recv.at[base + k], dev(k))
            for k in range(1, n)
        ]
        start_all(copies)
        return copies

    def add_sums(copies, value, base, n):
        wait_all(copies)
        for k in range(1, n):
            value = value + sums[base + k]
        return value

    heads = kv.shape[1] // HD
    group = width // kv.shape[1]

    def attend(first, last):
        scale = HD**-0.5
        mask = jnp.concatenate([valid[...]] * (steps * group), axis=0) > 0.5
        for j in range(first, last):
            lanes = slice(j * HD, (j + 1) * HD)
            query = queries[:, :, j * group * HD : (j + 1) * group * HD].astype(jnp.float32)
            q = [
                jnp.concatenate([query[n, :, i * HD : (i + 1) * HD] for i in range(group)], axis=0)
                for n in range(steps)
            ]
            old = lax.dot_general(
                jnp.concatenate(q, axis=0).astype(jnp.bfloat16),
                kv[:, lanes],
                (((1,), (1,)), ((), ())),
                preferred_element_type=jnp.float32,
            )
            old = jnp.where(mask, old * scale, -1e30)
            new = []
            for n in range(steps):
                k = jnp.concatenate([fresh[n, 0, :, lanes]] * group, axis=0)
                score = [
                    jnp.sum(q[i] * k, axis=1, keepdims=True) * scale
                    if n <= i
                    else jnp.full((q[i].shape[0], 1), -1e30, jnp.float32)
                    for i in range(steps)
                ]
                new.append(jnp.concatenate(score, axis=0))
            top = jnp.max(old, axis=1, keepdims=True)
            for e in new:
                top = jnp.maximum(top, e)
            old = jnp.exp(old - top)
            new = [jnp.exp(e - top) for e in new]
            whole = jnp.sum(old, axis=1, keepdims=True)
            for e in new:
                whole = whole + e
            inverse = 1.0 / whole
            prob = pltpu.roll(old * inverse, 1, 1).astype(jnp.bfloat16)
            y = jnp.dot(prob, kv[:, lanes], preferred_element_type=jnp.float32)
            for n in range(steps):
                v = jnp.concatenate([fresh[n, 1, :, lanes]] * (group * steps), axis=0)
                y = y + (new[n] * inverse).astype(jnp.bfloat16).astype(jnp.float32) * v
            for n in range(steps):
                for i in range(group):
                    at, row = j * group + i, (n * group + i) * 8
                    att[n, :, at * HD : (at + 1) * HD] = y[row : row + 8, :]

    sum_copies = send_sums(tile_sum, 0, n_fsdp, f_dev)
    attend(0, heads // 2)
    tile_sum = add_sums(sum_copies, tile_sum, 0, n_fsdp)
    sum_copies = send_sums(tile_sum, n_fsdp, n_group, g_dev)
    attend(heads // 2, heads)

    blend = (start[...].astype(jnp.float32) + att[0]).astype(jnp.bfloat16).astype(jnp.float32)
    factor = lax.rsqrt(jnp.sum(blend * blend, axis=1, keepdims=True) / width + norm_eps)
    for k in range(n_fsdp):
        cut = blend[:, k * depth : (k + 1) * depth]
        pieces[k, :8, :] = cut * factor * gain[k]
        pieces[k, 8:16, :] = cut
        for n in range(1, steps):
            pieces[k, (n + 1) * 8 : (n + 2) * 8, :] = att[n, :, k * depth : (k + 1) * depth]

    def piece_copies():
        return [
            remote(
                pieces.at[lax.rem(f + k, n_fsdp)], got_pieces.at[k], f_send.at[k], f_recv.at[k], f_dev(k)
            )
            for k in range(1, n_fsdp)
        ]

    start_all(piece_copies())
    got_pieces[0] = pieces[f]

    def joined(ref, a):
        at = pl.ds(a * 8, 8)
        blocks = [ref[lax.rem(f - b + n_fsdp, n_fsdp), at, :] for b in range(n_fsdp)]
        return jnp.concatenate(blocks, axis=0)

    def x_block(i):
        return x.at[i // x.shape[1], i % x.shape[1]]

    def x_along_tp(k):
        return remote(x_block(0), x_block(k), x_send.at[k], x_recv.at[k], z_dev(k))

    def x_along_rep(k):
        return [
            remote(x_block(k), x_block(i * n_tp + k), x_send.at[i * n_tp + k], x_recv.at[i * n_tp + k], r_dev(i))
            for i in range(1, n_rep)
        ]

    def x_start():
        start_all([x_along_tp(k) for k in range(1, n_tp)])
        start_all(x_along_rep(0))

    def x_forward(k):
        x_along_tp(k).wait()
        start_all(x_along_rep(k))

    def x_finish():
        for k in range(n_tp):
            wait_all(x_along_rep(k))

    tile_sum = add_sums(sum_copies, tile_sum, n_fsdp, n_group)
    clip = jnp.minimum(1.0, lax.rsqrt(jnp.sum(tile_sum, keepdims=True)))

    rate = 2.0 / FULL_WIDTH**0.5 / (1.0 - beta_one**adam_time)
    keep_m = rate * beta_one
    add_m = rate * (1.0 - beta_one)
    second_fix = 1.0 - beta_two**adam_time
    keep_v = beta_two / second_fix
    add_v = (1.0 - beta_two) / second_fix

    clip_m = add_m * clip
    clip_v = add_v * clip * clip

    def update(s, j, slot):
        def rows_at(b, carry):
            at = pl.ds(pl.multiple_of(b * SUB, SUB), SUB)
            grad = weights[s, j, at, :].astype(jnp.float32)
            first = keep_m * slots[slot, 1, at, :] + clip_m * grad
            second = keep_v * slots[slot, 2, at, :] + clip_v * (grad * grad)
            under = second * lax.rsqrt(second) + adam_eps
            inverse = pl.reciprocal(under, approx=True)
            inverse = inverse * (2.0 - under * inverse)
            new = slots[slot, 0, at, :] - first * inverse
            weights[s, j, at, :] = new.astype(jnp.bfloat16)
            return carry

        lax.fori_loop(0, depth // SUB, rows_at, 0, unroll=2)


    def core_copy(j):
        return remote(core_out.at[j], core_in.at[j], core_send.at[j], core_recv.at[j], sibling)

    def y_copy(j, k):
        there = lax.rem(m + k, members)
        return remote(
            y_out.at[j, there], y_in.at[j, k - 1], y_send.at[j, k - 1], y_recv.at[j, k - 1], m_dev(k)
        )

    def h_copy(j, k):
        return remote(
            hid.at[j, c, m], hid.at[j, c, m], h_send.at[j, k - 1], h_recv.at[j, k - 1], m_dev(k)
        )

    def h_arrival(j, k):
        there = lax.rem(m - k + members, members)
        return remote(
            hid.at[j, c, m], hid.at[j, c, there], h_send.at[j, k - 1], h_recv.at[j, k - 1], m_dev(k)
        )

    def hc_copy(j):
        return remote(hid.at[j, c], hid.at[j, c], hc_send.at[j], hc_recv.at[j], sibling)

    def hc_arrival(j):
        return remote(hid.at[j, c], hid.at[j, 1 - c], hc_send.at[j], hc_recv.at[j], sibling)

    def multiply(j):
        theirs = x[1 - c].reshape(half, depth)
        mine = x[c].reshape(half, depth)
        both = jnp.concatenate([theirs, mine], axis=0)
        for a in range(2):
            y = jnp.dot(both, weights[a, j], preferred_element_type=jnp.float32)
            core_out[j, :, a * TILE : (a + 1) * TILE] = y[:half].astype(jnp.bfloat16)
            own[j, :, a * TILE : (a + 1) * TILE] = y[half:]
        core_copy(j).start()

    def add_core(j):
        core_copy(j).wait()
        y = own[j] + core_in[j].astype(jnp.float32)
        own[j] = y
        y_out[j] = y.astype(jnp.bfloat16).reshape(members, part, 2 * TILE)
        for k in range(1, members):
            y_copy(j, k).start()

    def second_stage(j):
        y = own[j, pl.ds(pl.multiple_of(m * part, part), part), :]
        for k in range(1, members):
            y_copy(j, k).wait()
            y = y + y_in[j, k - 1].astype(jnp.float32)
        gate, upper = y[:, :TILE], y[:, TILE:]
        hid[j, c, m] = (gate * jax.nn.sigmoid(gate) * upper).astype(jnp.bfloat16)
        for k in range(1, members):
            h_copy(j, k).start()

    def third_stage(j):
        for k in range(1, members):
            h_copy(j, k).wait_send()
            h_arrival(j, k).wait_recv()
        hc_copy(j).start()

    def fourth_stage(j):
        hc_copy(j).wait_send()
        hc_arrival(j).wait_recv()
        acc[...] += lax.dot_general(
            hid[j].reshape(2 * half, TILE),
            weights[2, j],
            (((1,), (1,)), ((), ())),
            preferred_element_type=jnp.float32,
        )

    def after(j, first, stage):
        @pl.when(first <= j)
        def _():
            stage(j - first)

    def before(j, first, stage):
        @pl.when(j < tiles - first)
        def _():
            stage(j + first)

    def update_pair(j, carry):
        for a in range(2):
            wait_all(pair_copies(a, j))
            update(a, j, lax.rem(2 * j + a, SLOTS))

            @pl.when(j + SLOTS // 2 < tiles)
            def _():
                start_all(pair_copies(a, j + SLOTS // 2))

            @pl.when(j + SLOTS // 2 >= tiles)
            def _():
                start_all(down_copies(2 * (j + SLOTS // 2 - tiles) + a))

        @pl.when(j == 0)
        def _():
            wait_all(piece_copies())
            x[0, 0] = joined(got_pieces, 0).astype(jnp.bfloat16)
            mixed[...] = joined(got_pieces, 1)
            x_start()

        for k in range(1, n_tp):

            @pl.when(j == min(k, LAG))
            def _(k=k):
                x_forward(k)

        @pl.when(j == LAG)
        def _():
            x_finish()

        after(j, LAG, multiply)
        after(j, LAG + 1, add_core)
        after(j, LAG + 2, second_stage)
        after(j, LAG + 3, third_stage)
        return carry

    def update_down(j, carry):
        wait_all(down_copies(j))
        update(2, j, lax.rem(2 * tiles + j, SLOTS))

        @pl.when(j + SLOTS < tiles)
        def _():
            start_all(down_copies(j + SLOTS))

        before(j, tiles - LAG, multiply)
        before(j, tiles - LAG - 1, add_core)
        before(j, tiles - LAG - 2, second_stage)
        before(j, tiles - LAG - 3, third_stage)
        after(j, 2, fourth_stage)
        return carry

    def looped(stage, first, last):
        def body(j, carry):
            stage(j)
            return carry

        lax.fori_loop(first, last, body, 0)

    for step in range(steps):
        acc[...] = jnp.zeros_like(acc)
        if step == 0:
            lax.fori_loop(0, tiles, update_pair, 0)
            lax.fori_loop(0, tiles, update_down, 0)
            looped(fourth_stage, tiles - 2, tiles)
        else:

            def first_stage(j):
                multiply(j)
                after(j, 1, add_core)

            looped(first_stage, 0, tiles)
            add_core(tiles - 1)
            looped(second_stage, 0, tiles)
            looped(third_stage, 0, tiles)
            looped(fourth_stage, 0, tiles)

        rows_of = acc.shape[0] // n_group

        def own_block(i):
            return acc[i * rows_of : (i + 1) * rows_of, :]

        def down_along_rep(k):
            return [
                remote(down_out.at[i], down_in.at[i], d_send.at[i], d_recv.at[i], r_dev(n_rep - i // n_tp))
                for i in range(n_tp + k, n_group, n_tp)
            ]

        def down_along_tp(k):
            return remote(down_out.at[k], down_in.at[k], d_send.at[k], d_recv.at[k], z_dev(n_tp - k))

        order = list(range(1, n_tp)) + [0]
        for k in order:
            for i in range(n_tp + k, n_group, n_tp):
                down_out[i] = own_block(i).astype(jnp.bfloat16)
            start_all(down_along_rep(k))
        summed = None
        for k in order:
            wait_all(down_along_rep(k))
            summed = own_block(k)
            for i in range(n_tp + k, n_group, n_tp):
                summed = summed + down_in[i].astype(jnp.float32)
            if k > 0:
                down_out[k] = summed.astype(jnp.bfloat16)
                down_along_tp(k).start()
        for k in range(1, n_tp):
            down_along_tp(k).wait()
            summed = summed + down_in[k].astype(jnp.float32)
        rows = (mixed[...] + summed).astype(jnp.bfloat16).astype(jnp.float32)

        if step < steps - 1:
            blend = (rows + joined(got_pieces, 2 + step)).astype(jnp.bfloat16).astype(jnp.float32)
            mixed[...] = blend
            local = jnp.sum(blend * blend, axis=1, keepdims=True)
            squares[0] = jnp.broadcast_to(local, squares.shape[1:])
            copies = []
            for k in range(1, n_fsdp):
                copy = remote(squares.at[0], squares.at[k], f_send.at[k], f_recv.at[k], f_dev(k))
                copy.start()
                copies.append(copy)
            for copy in copies:
                copy.wait()
            whole = squares[0]
            for k in range(1, n_fsdp):
                whole = whole + squares[k]
            factor = lax.rsqrt(whole[:, :1] / (depth * n_fsdp) + norm_eps)
            x[0, 0] = (mixed[...] * factor * gain[f]).astype(jnp.bfloat16)
            x_start()
            for k in range(1, n_tp):
                x_forward(k)
            x_finish()
        else:
            for k in range(n_fsdp):
                fin_out[k] = rows[k * 8 : (k + 1) * 8, :]
            copies = []
            for k in range(1, n_fsdp):
                there = lax.rem(f + k, n_fsdp)
                copy = remote(fin_out.at[there], fin_in.at[k], f_send.at[k], f_recv.at[k], f_dev(k))
                copy.start()
                copies.append(copy)
            out[f] = fin_out[f]
            for k in range(1, n_fsdp):
                copies[k - 1].wait()
                out[lax.rem(f - k + n_fsdp, n_fsdp)] = fin_in[k]


def shards(
    gate_up_master,
    gate_up_moment,
    gate_up_second,
    gate_up_grad,
    down_master,
    down_moment,
    down_second,
    down_grad,
    norm_gain,
    start_rows,
    queries,
    new_kv,
    kv_pool,
    page_table,
    cache_len,
):
    n_rep, n_fsdp, n_tp = (lax.axis_size(a) for a in ("rep", "fsdp", "tp"))
    n_group = n_rep * n_tp
    depth, cols = down_grad.shape
    local_rows, width = start_rows.shape
    steps = queries.shape[0]
    tiles = cols // TILE
    members = n_fsdp // 2
    block = local_rows * n_fsdp
    all_rows = block * n_group
    half = all_rows // 2

    pages, page, _, kv_width = kv_pool.shape
    kv = kv_pool
    fresh = new_kv.astype(jnp.float32).transpose(0, 2, 1, 3)
    gain = norm_gain.reshape(n_fsdp, 1, depth)

    bf16, f32 = jnp.bfloat16, jnp.float32
    dma = pltpu.SemaphoreType.DMA
    final = pl.pallas_call(
        functools.partial(block_kernel, n_rep, n_fsdp, n_tp, page),
        out_shape=jax.ShapeDtypeStruct((n_fsdp, local_rows, depth), f32),
        in_specs=[pl.BlockSpec(memory_space=pl.ANY)] * 8 + [pl.BlockSpec(memory_space=pltpu.VMEM)] * 7,
        out_specs=pl.BlockSpec(memory_space=pltpu.VMEM),
        scratch_shapes=[
            pltpu.VMEM((3, tiles, depth, TILE), bf16),
            pltpu.VMEM((SLOTS, 3, depth, TILE), f32),
            pltpu.VMEM((2 * pages * page, kv_width), bf16),
            pltpu.VMEM((local_rows, 2 * pages * page), f32),
            pltpu.VMEM((steps, local_rows, width), f32),
            pltpu.VMEM((n_fsdp, (steps + 1) * local_rows, depth), f32),
            pltpu.VMEM((n_fsdp, (steps + 1) * local_rows, depth), f32),
            pltpu.VMEM((n_fsdp + n_group, 8, 128), f32),
            pltpu.VMEM((2, n_group // 2, block, depth), bf16),
            pltpu.VMEM((tiles, half, 2 * TILE), f32),
            pltpu.VMEM((tiles, half, 2 * TILE), bf16),
            pltpu.VMEM((tiles, half, 2 * TILE), bf16),
            pltpu.VMEM((tiles, members, half // members, 2 * TILE), bf16),
            pltpu.VMEM((tiles, members - 1, half // members, 2 * TILE), bf16),
            pltpu.VMEM((tiles, 2, members, half // members, TILE), bf16),
            pltpu.VMEM((all_rows, depth), f32),
            pltpu.VMEM((n_group, block, depth), bf16),
            pltpu.VMEM((n_group, block, depth), bf16),
            pltpu.VMEM((n_fsdp, block, 128), f32),
            pltpu.VMEM((block, depth), f32),
            pltpu.VMEM((n_fsdp, local_rows, depth), f32),
            pltpu.VMEM((n_fsdp, local_rows, depth), f32),
            dma((3, tiles)),
            dma((SLOTS, 3)),
            dma((n_fsdp,)),
            dma((n_fsdp,)),
            dma((n_fsdp + n_group,)),
            dma((n_fsdp + n_group,)),
            dma((n_group,)),
            dma((n_group,)),
            dma((tiles,)),
            dma((tiles,)),
            dma((tiles, members - 1)),
            dma((tiles, members - 1)),
            dma((tiles, members - 1)),
            dma((tiles, members - 1)),
            dma((tiles,)),
            dma((tiles,)),
            dma((n_group,)),
            dma((n_group,)),
        ],
        compiler_params=pltpu.CompilerParams(
            collective_id=0, has_side_effects=True, vmem_limit_bytes=60 * 2**20
        ),
        cost_estimate=pl.CostEstimate(
            flops=2 * steps * all_rows * 3 * depth * cols,
            bytes_accessed=3 * depth * cols * 14,
            transcendentals=3 * depth * cols,
        ),
        name="update_and_decode",
    )(
        gate_up_master,
        gate_up_moment,
        gate_up_second,
        gate_up_grad,
        down_master,
        down_moment,
        down_second,
        down_grad,
        gain,
        start_rows,
        queries,
        kv,
        page_table,
        cache_len.reshape(local_rows, 1),
        fresh,
    )
    return final.transpose(1, 0, 2).reshape(local_rows, width).astype(jnp.bfloat16)


def solution(mesh):
    in_specs = (
        P(None, "fsdp", ("rep", "tp")),
        P(None, "fsdp", ("rep", "tp")),
        P(None, "fsdp", ("rep", "tp")),
        P(None, "fsdp", ("rep", "tp")),
        P("fsdp", ("rep", "tp")),
        P("fsdp", ("rep", "tp")),
        P("fsdp", ("rep", "tp")),
        P("fsdp", ("rep", "tp")),
        P(),
        P(("rep", "fsdp", "tp"), None),
        P(None, ("rep", "fsdp", "tp"), None),
        P(None, ("rep", "fsdp", "tp"), None, None),
        P(("rep", "fsdp", "tp"), None, None, None),
        P(("rep", "fsdp", "tp"), None),
        P(("rep", "fsdp", "tp")),
    )
    out_specs = P(("rep", "fsdp", "tp"), None)
    return jax.shard_map(shards, mesh=mesh, in_specs=in_specs, out_specs=out_specs, check_vma=False)
```
